128 devices in a mesh: lat: 64 (over z, y, x), obs: 2 (over core).
Axes of the slice: x: 4, y: 4, z: 4, core: 2. Of those that a mesh axis runs over, the one named last changes fastest.
Arguments:
- control: bfloat16 [2, 64, 512, 3072], P(None, 'obs', 'lat'), may hold values from -8 to 8
- zonal_scales: float32 [4], replicated, may hold values from 1.5 to 360, as said below
- zonal_heights: float32 [4], replicated, may hold values from 0.25 to 0.75
- meridional_scales: float32 [4], replicated, may hold values from 0.8 to 180, as said below
- meridional_heights: float32 [4], replicated, may hold values from 0.25 to 0.75
- vertical_map: bfloat16 [2, 64, 64], replicated, may hold values from -0.75 to 0.75
- send_blocks: int32 [64, 2, 2, 2], P('lat', 'obs'), may hold values from 0 to 63
- report_slot: int32 [64, 2, 2048], P('lat', 'obs'), may hold values from 0 to 3
- report_level: int32 [64, 2, 2048], P('lat', 'obs'), may hold values from 0 to 127
- report_corner: int32 [64, 2, 4, 2048], P('lat', 'obs'), may hold values from 0 to 191, as said below
- report_weight: float32 [64, 2, 4, 2048], P('lat', 'obs'), may hold values from 0 to 1, as said below
- innovation: float32 [64, 2, 2048], P('lat', 'obs'), may hold values from -6 to 6
- report_precision: float32 [64, 2, 2048], P('lat', 'obs'), may hold values from 1 to 4
Outputs:
- weighted_departure: float32 [64, 2, 2048], P('lat', 'obs')
- control_gradient: float32 [2, 64, 512, 3072], P(None, 'obs', 'lat')
The draws below stay inside these ranges and needn't reach their ends.
Inputs may be any that keep to these rules, and one draw needn't show every extreme that they name: `report_corner`: the corners of an observation are q, q + 1, q + 48, q + 49 in this order, with q // 48 < 3 and q % 48 < 47. `report_weight`: nonnegative bilinear weights whose four values sum to one, in the corner order of report_corner. `zonal_scales`: positive length scales. `meridional_scales`: positive length scales.
All inputs are finite; a program needn't handle non-finite values.
Results may differ from the reference program's by a relative error of at most 0.009.
Values may be sent and summed in bfloat16 or wider, within the bound.
No kernel may reach another device: no remote copies, remote signals or barrier semaphores. Data moves between devices by JAX's collectives and lax.ppermute only.
A program may use at most 128 MiB of HBM per device.

```python
import math
import jax
import jax.numpy as jnp
import numpy as np
from jax import lax

V = 2
L = 64
NX = 3072
REPORTS = 2048
SLOTS = 2
BR = 4
NY = 512
XW = 48
YB = 256
NBLK = 64
N_LAT = 64
N_OBS = 2


def length_scales(key, lows, highs):
    first, second = jax.random.split(key)
    order = jax.random.permutation(first, 4)
    unit = jax.random.uniform(second, (4,), jnp.float32)
    bottom = jnp.log(jnp.array(lows, jnp.float32))
    top = jnp.log(jnp.array(highs, jnp.float32))
    return jnp.exp(bottom + unit * (top - bottom))[order]


def draw_control(key, part):
    key = jax.random.fold_in(key, 21)
    first, second, third = jax.random.split(key, 3)
    wave_number = jax.random.randint(second, (V, L, NY, 1), 40, 71)
    phase = jax.random.uniform(third, (V, L, NY, 1), jnp.float32, 0.0, 2.0 * math.pi)
    cells = jnp.arange(NX, dtype=jnp.int32).reshape(1, 1, 1, NX)
    turn = (wave_number * cells % NX).astype(jnp.float32) * (2.0 * math.pi / NX)
    wave = jnp.cos(turn + phase)
    noise = jnp.clip(jax.random.normal(first, (V, L, NY, NX), jnp.float32), -6.0, 6.0)
    result = noise + wave
    return result.astype(jnp.bfloat16)


def draw_zonal_scales(key, part):
    key = jax.random.fold_in(key, 5)
    return length_scales(key, [2.0, 17.0, 23.0, 90.0], [6.0, 23.0, 30.0, 300.0])


def draw_meridional_scales(key, part):
    key = jax.random.fold_in(key, 9)
    return length_scales(key, [1.0, 3.5, 14.0, 55.0], [2.2, 8.0, 32.0, 150.0])


def draw_report_corner(key, part):
    key = jax.random.fold_in(key, 13)
    first, second = jax.random.split(key)
    row = jax.random.randint(first, (N_LAT, N_OBS, 1, REPORTS), 0, BR - 1)
    cell = jax.random.randint(second, (N_LAT, N_OBS, 1, REPORTS), 0, XW - 1)
    base = row * XW + cell
    base = base.at[:, :, :, 0].set((BR - 2) * XW + XW - 2)
    base = base.at[:, :, :, 1].set(0)
    offsets = jnp.array([0, 1, XW, XW + 1], jnp.int32).reshape(1, 1, 4, 1)
    return (base + offsets).astype(jnp.int32)


def draw_report_weight(key, part):
    key = jax.random.fold_in(key, 17)
    first, second = jax.random.split(key)
    across = jax.random.uniform(first, (N_LAT, N_OBS, 1, REPORTS), jnp.float32)
    upward = jax.random.uniform(second, (N_LAT, N_OBS, 1, REPORTS), jnp.float32)
    return jnp.concatenate([(1.0 - across) * (1.0 - upward), across * (1.0 - upward), (1.0 - across) * upward, across * upward], axis=2)


def touch_ends(values, own_key, smallest, top_value):
    place = [jax.random.randint(jax.random.fold_in(own_key, axis), (), 0, length) for axis, length in enumerate(values.shape)]
    main_axis = values.shape.index(max(values.shape))
    next_to = place[:main_axis] + [(place[main_axis] + 1) % values.shape[main_axis]] + place[main_axis + 1:]
    return values.at[tuple(place)].set(smallest).at[tuple(next_to)].set(top_value)


def block_levels(stream_key, extent, pieces, smallest, high):
    gain = 1.0
    for axis_at, parts in pieces:
        steps = jax.random.uniform(jax.random.fold_in(jax.random.fold_in(stream_key, 6), axis_at), (parts,), jnp.float32, smallest / len(pieces), high / len(pieces))
        gain = gain * jnp.repeat(jnp.exp(steps), extent[axis_at] // parts).reshape((-1,) + (1,) * (len(extent) - 1 - axis_at))
    return gain


def cumulative_ranks(amount, slope):
    portions = [(1 << 20) // math.isqrt(rank ** slope) + 1 for rank in range(1, amount + 1)]
    deviation = 1 + sum(portions) // (1 << 30)
    return np.cumsum(np.array([max(1, weight // deviation) for weight in portions]))


def ranked_ids(stream_key, extent, count, slope):
    table = cumulative_ranks(count, slope)
    lot = jax.random.randint(jax.random.fold_in(stream_key, 1), extent, 0, int(table[count - 1]))
    grade = jnp.searchsorted(jnp.asarray(table, jnp.int32), lot, side="right")
    return jax.random.permutation(jax.random.fold_in(stream_key, 2), count)[grade].astype(jnp.int32)


def centred(own_key, dims, width, most, pieces=(), kind=jnp.bfloat16):
    gain = block_levels(own_key, dims, pieces, -0.22, 0.18) if pieces else 1.0
    values = jax.random.normal(own_key, dims, jnp.float32) * width * gain
    return jnp.minimum(jnp.maximum(values, -most), most).astype(kind)


def setup_inputs(seed: int = 0) -> dict:
    key_list = jax.random.split(jax.random.key(seed), 14)
    control = draw_control(jax.random.fold_in(key_list[13], 71), 0)
    zonal_scales = draw_zonal_scales(jax.random.fold_in(key_list[13], 71), 0)
    zonal_heights = jnp.clip(jax.random.uniform(key_list[2], (4,), jnp.float32, 0.25, 0.75), 0.25, 0.75)
    meridional_scales = draw_meridional_scales(jax.random.fold_in(key_list[13], 71), 0)
    meridional_heights = jnp.clip(jax.random.uniform(key_list[4], (4,), jnp.float32, 0.25, 0.75), 0.25, 0.75)
    vertical_map = centred(key_list[5], (V, L, L), L ** -0.5, 0.75)
    send_blocks = touch_ends(jax.random.randint(key_list[6], (N_LAT, N_OBS, N_OBS, SLOTS), 0, NBLK), jax.random.fold_in(key_list[6], 1), 0, NBLK - 1).astype(jnp.int32)
    report_slot = touch_ends(ranked_ids(key_list[7], (N_LAT, N_OBS, REPORTS), N_OBS * SLOTS, 2), jax.random.fold_in(key_list[7], 3), 0, (N_OBS * SLOTS) - 1).astype(jnp.int32)
    report_level = touch_ends(jax.random.randint(key_list[8], (N_LAT, N_OBS, REPORTS), 0, V * L), jax.random.fold_in(key_list[8], 1), 0, (V * L) - 1).astype(jnp.int32)
    report_corner = draw_report_corner(jax.random.fold_in(key_list[13], 71), 0)
    report_weight = draw_report_weight(jax.random.fold_in(key_list[13], 71), 0)
    innovation = centred(key_list[11], (N_LAT, N_OBS, REPORTS), 1.0, 6.0, ((0, 64), (1, 2)), jnp.float32)
    report_precision = jnp.clip(jnp.exp(math.log(4.0) - 1.3862944 * jax.random.uniform(key_list[12], (N_LAT, N_OBS, REPORTS), jnp.float32) ** block_levels(key_list[12], (N_LAT, N_OBS, REPORTS), ((0, 64), (1, 2)), -0.2, 0.2)), 1.0, 4.0)
    return {"control": control, "zonal_scales": zonal_scales, "zonal_heights": zonal_heights, "meridional_scales": meridional_scales, "meridional_heights": meridional_heights, "vertical_map": vertical_map, "send_blocks": send_blocks, "report_slot": report_slot, "report_level": report_level, "report_corner": report_corner, "report_weight": report_weight, "innovation": innovation, "report_precision": report_precision}


def profile(distance, scales, heights):
    total = jnp.zeros(distance.shape, jnp.float32)
    for member in range(4):
        scale = scales[member]
        total = total + heights[member] * jnp.exp(-distance * distance / (2.0 * scale * scale)) / jnp.sqrt(math.sqrt(math.pi) * scale)
    return total

def reference(control, zonal_scales, zonal_heights, meridional_scales, meridional_heights, vertical_map, send_blocks, report_slot, report_level, report_corner, report_weight, innovation, report_precision):
    offsets = jnp.arange(NX)
    cycle = jnp.minimum(offsets, NX - offsets).astype(jnp.float32)
    kernel = lax.optimization_barrier(profile(cycle, zonal_scales, zonal_heights).astype(jnp.bfloat16)).astype(jnp.float32)
    spectrum = jnp.fft.rfft(kernel)
    places = jnp.arange(NY)
    apart = jnp.abs(places[:, None] - places[None, :]).astype(jnp.float32)
    meridional = profile(apart, meridional_scales, meridional_heights).astype(jnp.bfloat16)

    def along_zonal(plane):
        return jnp.fft.irfft(jnp.fft.rfft(plane.astype(jnp.float32), axis=-1) * spectrum, n=NX, axis=-1)

    def forward_plane(plane):
        smoothed = along_zonal(plane).astype(jnp.bfloat16)
        return jnp.dot(meridional, smoothed, preferred_element_type=jnp.float32).astype(jnp.bfloat16)

    def backward_plane(plane):
        mixed = jnp.dot(meridional.T, plane, preferred_element_type=jnp.float32).astype(jnp.bfloat16)
        return along_zonal(mixed).astype(jnp.float32)
    increments = []
    for variable in range(V):
        lined = lax.map(forward_plane, control[variable])
        mixed = jnp.dot(vertical_map[variable], lined.reshape(L, NY * NX), preferred_element_type=jnp.float32)
        increments.append(mixed.reshape(L, NY, NX))
    increment = jnp.stack(increments)
    lat_ids = jnp.arange(N_LAT).reshape(N_LAT, 1, 1, 1).astype(jnp.int32)
    owner_ids = jnp.arange(N_OBS).reshape(1, N_OBS, 1, 1).astype(jnp.int32)
    slot = report_slot[:, :, None, :]
    anchor = slot // SLOTS
    chosen = send_blocks[lat_ids, anchor, owner_ids, slot % SLOTS]
    code = report_level[:, :, None, :]
    variable_ids = code // L
    level_ids = code % L
    row_ids = anchor * YB + chosen * BR + report_corner // XW
    column_ids = lat_ids * XW + report_corner % XW
    values = increment[variable_ids, level_ids, row_ids, column_ids]
    model_value = lax.optimization_barrier(jnp.sum(report_weight * values, axis=2))
    departure = report_precision * (model_value - innovation)
    pushes = report_weight * departure[:, :, None, :]
    adjoint = jnp.zeros((V, L, NY, NX), jnp.float32).at[variable_ids, level_ids, row_ids, column_ids].add(pushes)
    gradients = []
    for variable in range(V):
        lifted = jnp.dot(vertical_map[variable].astype(jnp.float32).T, adjoint[variable].reshape(L, NY * NX), precision=lax.Precision.HIGHEST)
        lifted = lifted.astype(jnp.bfloat16).reshape(L, NY, NX)
        gradients.append(lax.map(backward_plane, lifted))
    return (departure, jnp.stack(gradients))
```

```python
import math

import jax
import jax.numpy as jnp
from jax import lax
from jax.experimental import pallas as pl
from jax.experimental.pallas import tpu as pltpu
from jax.sharding import PartitionSpec as P

NV = 2
LH = 32
NX = 3072
NY = 512
XW = 48
BAND = 8
NLAT = 64
GROUP = 8 * XW
LANES = LH * XW
TILE = 256
SLAB = NX + 2 * TILE
WIDE = 3 * TILE
STEPS = NX // WIDE
ROWS = 16
COLS = ROWS * XW
REPORTS = 2048
MIB = 2**20

PIECES = (
    ((0, 48), (1, 96), (2, 128)),
    ((2, 16), (3, 64), (4, 112), (5, 128)),
    ((5, 32), (6, 80), (7, 128)),
)


def gaussians(distance, scales, heights):
    total = jnp.zeros(distance.shape, jnp.float32)
    for member in range(4):
        scale = scales[member]
        total = total + heights[member] * jnp.exp(
            -distance * distance / (2.0 * scale * scale)
        ) / jnp.sqrt(math.sqrt(math.pi) * scale)
    return total


def fill_slab(scales_ref, heights_ref, slab_ref):
    shape = (8, NX)
    offset = jnp.abs(
        lax.broadcasted_iota(jnp.int32, shape, 1) - lax.broadcasted_iota(jnp.int32, shape, 0)
    )
    distance = jnp.minimum(offset, NX - offset).astype(jnp.float32)
    scales = [jnp.full((1, 128), scales_ref[m], jnp.float32)[:, :1] for m in range(4)]
    heights = [jnp.full((1, 128), heights_ref[m], jnp.float32)[:, :1] for m in range(4)]
    base = gaussians(distance, scales, heights)
    for pair in range(TILE // 16):
        upper = base if pair == 0 else pltpu.roll(base, 16 * pair, 1)
        lower = pltpu.roll(base, 16 * pair + 8, 1)
        both = jnp.concatenate([upper, lower], axis=0).astype(jnp.bfloat16)
        slab_ref[16 * pair : 16 * pair + 16, :NX] = both
        slab_ref[16 * pair : 16 * pair + 16, NX:] = both[:, : SLAB - NX]


def zonal_columns(slab_ref, step):
    parts = []
    for block in range(NX // TILE):
        start = lax.rem(WIDE * step + (NX - TILE * block), NX)
        parts.append(slab_ref[:, pl.ds(pl.multiple_of(start, TILE), WIDE)])
    return jnp.concatenate(parts, axis=0)


def pick(tiles, shift, lane):
    result = []
    for tile, pieces in enumerate(PIECES):
        low = 128 * tile
        value = tiles[(pieces[-1][0] - shift) % 8][:, low : low + 128]
        for block, end in pieces[-2::-1]:
            value = jnp.where(lane < end, tiles[(block - shift) % 8][:, low : low + 128], value)
        result.append(value)
    return jnp.concatenate(result, axis=1)


def forward_zonal_kernel(scales_ref, heights_ref, field_ref, out_ref, slab_ref, acc_ref):
    step = pl.program_id(0)

    @pl.when(step == 0)
    def _():
        fill_slab(scales_ref, heights_ref, slab_ref)

    acc_ref[...] = jnp.dot(
        field_ref[...], zonal_columns(slab_ref, step), preferred_element_type=jnp.float32
    )
    lane = lax.broadcasted_iota(jnp.int32, (16, 128), 1)
    for strips in range(2):
        for group in range(LH // 8):
            turned = []
            for j in range(8):
                row = (group * 8 + j) * BAND
                both = jnp.concatenate(
                    [
                        acc_ref[v * LH * BAND + row : v * LH * BAND + row + BAND,
                                strips * GROUP : (strips + 1) * GROUP]
                        for v in range(NV)
                    ],
                    axis=0,
                )
                turned.append(both if j == 0 else pltpu.roll(both, XW * j, 1))
            for i in range(8):
                out_ref[strips * 8 + i, :, group * GROUP : (group + 1) * GROUP] = pick(
                    turned, i, lane
                ).astype(jnp.bfloat16)


def forward_zonal(field, scales, heights):
    return pl.pallas_call(
        forward_zonal_kernel,
        grid=(STEPS,),
        in_specs=[
            pl.BlockSpec(memory_space=pltpu.SMEM),
            pl.BlockSpec(memory_space=pltpu.SMEM),
            pl.BlockSpec((NV * LH * BAND, NX), lambda s: (0, 0)),
        ],
        out_specs=[
            pl.BlockSpec((NLAT // STEPS, 16, LANES), lambda s: (s, 0, 0)),
            pl.BlockSpec((TILE, SLAB), lambda s: (0, 0)),
        ],
        out_shape=[
            jax.ShapeDtypeStruct((NLAT, 16, LANES), jnp.bfloat16),
            jax.ShapeDtypeStruct((TILE, SLAB), jnp.bfloat16),
        ],
        scratch_shapes=[pltpu.VMEM((NV * LH * BAND, WIDE), jnp.float32)],
        compiler_params=pltpu.CompilerParams(vmem_limit_bytes=48 * MIB),
        cost_estimate=pl.CostEstimate(
            flops=2 * NV * LH * BAND * NX * NX, bytes_accessed=8 * MIB, transcendentals=10**5
        ),
        name="forward_zonal",
    )(scales, heights, field)


def backward_zonal_kernel(slab_ref, lines_ref, out_ref, field_ref):
    step = pl.program_id(0)

    @pl.when(step == 0)
    def _():
        lane = lax.broadcasted_iota(jnp.int32, (16, 128), 1)

        def fill(strips, carry):
            for group in range(LH // 8):
                tiles = [
                    lines_ref[strips * 8 + i, :, group * GROUP : (group + 1) * GROUP].astype(
                        jnp.float32
                    )
                    for i in range(8)
                ]
                for j in range(8):
                    level = pick(tiles, j, lane)
                    if j:
                        level = pltpu.roll(level, GROUP - XW * j, 1)
                    row = (group * 8 + j) * 16
                    start = pl.multiple_of(strips * GROUP, 128)
                    field_ref[row : row + 16, pl.ds(start, GROUP)] = level.astype(jnp.bfloat16)
            return carry

        lax.fori_loop(0, NLAT // 8, fill, 0)

    acc = jnp.dot(
        field_ref[...], zonal_columns(slab_ref, step), preferred_element_type=jnp.float32
    )
    for level in range(LH):
        for v in range(NV):
            row = (level * NV + v) * BAND
            out_ref[v, level] = acc[row : row + BAND]


def backward_zonal(slab, lines):
    return pl.pallas_call(
        backward_zonal_kernel,
        grid=(STEPS,),
        in_specs=[
            pl.BlockSpec((TILE, SLAB), lambda s: (0, 0)),
            pl.BlockSpec((NLAT, 16, LANES), lambda s: (0, 0, 0)),
        ],
        out_specs=pl.BlockSpec((NV, LH, BAND, WIDE), lambda s: (0, 0, 0, s)),
        out_shape=jax.ShapeDtypeStruct((NV, LH, BAND, NX), jnp.float32),
        scratch_shapes=[pltpu.VMEM((NV * LH * BAND, NX), jnp.bfloat16)],
        compiler_params=pltpu.CompilerParams(vmem_limit_bytes=48 * MIB),
        cost_estimate=pl.CostEstimate(
            flops=2 * NV * LH * BAND * NX * NX, bytes_accessed=12 * MIB, transcendentals=0
        ),
        name="backward_zonal",
    )(slab, lines)


def stencil_kernel(where_ref, mine_ref, other_ref, map_ref, stencil_ref, level_ref):
    strip_turn, half = where_ref[0], where_ref[1]
    shape = (LH, 2 * LH)
    slot = lax.broadcasted_iota(jnp.int32, shape, 0)
    level = (slot // 8) * 8 + lax.rem(lax.rem(slot, 8) + (8 - strip_turn), 8) + LH * half
    order = (lax.broadcasted_iota(jnp.int32, shape, 1) == level).astype(jnp.bfloat16)
    for owner, ref in enumerate((mine_ref, other_ref)):
        code = ref[1:2, :].astype(jnp.int32)
        for v in range(NV):
            rows = lax.broadcasted_iota(jnp.int32, (2 * LH, REPORTS), 0) + 2 * LH * v
            hot = (rows == code).astype(jnp.float32).astype(jnp.bfloat16)
            picked = lax.dot_general(
                map_ref[v], hot, (((0,), (0,)), ((), ())), preferred_element_type=jnp.float32
            ).astype(jnp.bfloat16)
            level_ref[owner, v * LH : (v + 1) * LH, :] = jnp.dot(
                order, picked, preferred_element_type=jnp.float32
            ).astype(jnp.bfloat16)
        base = ref[0:1, :] * float(4 * XW)
        points = [(base + ref[2 + c : 3 + c, :]).astype(jnp.int32) for c in range(4)]
        weights = [ref[6 + c : 7 + c, :] for c in range(4)]

        def fill(tile, carry):
            start = pl.multiple_of(tile * 16, 16)
            column = lax.broadcasted_iota(jnp.int32, (16, REPORTS), 0) + start
            value = jnp.zeros((16, REPORTS), jnp.float32)
            for c in range(4):
                value = jnp.where(column == points[c], weights[c], value)
            stencil_ref[owner, pl.ds(start, 16), :] = value.astype(jnp.bfloat16)
            return carry

        lax.fori_loop(0, COLS // 16, fill, 0)


def stencils(where, mine, other, vertical_map):
    return pl.pallas_call(
        stencil_kernel,
        in_specs=[pl.BlockSpec(memory_space=pltpu.SMEM)] + [pl.BlockSpec(memory_space=pltpu.VMEM)] * 3,
        out_shape=[
            jax.ShapeDtypeStruct((2, COLS, REPORTS), jnp.bfloat16),
            jax.ShapeDtypeStruct((2, NV * LH, REPORTS), jnp.bfloat16),
        ],
        compiler_params=pltpu.CompilerParams(vmem_limit_bytes=40 * MIB),
        cost_estimate=pl.CostEstimate(
            flops=10**8, bytes_accessed=8 * MIB, transcendentals=0
        ),
        name="stencils",
    )(where, mine, other, vertical_map)


def observe_kernel(rows_ref, lines_ref, stencil_ref, level_ref, out_ref, pick_ref, grid_ref):
    lines = lines_ref[...].reshape(NLAT * 16, LANES)
    mixed = jnp.dot(rows_ref[...], lines, preferred_element_type=jnp.float32)
    mixed = mixed.astype(jnp.bfloat16).astype(jnp.float32)
    for level in range(LH):
        pick_ref[level * 64 : (level + 1) * 64, :XW] = mixed[:, level * XW : (level + 1) * XW]
    for owner in range(2):
        for v in range(NV):
            for row in range(ROWS):
                start = (owner * NV + v) * ROWS + row
                column = owner * COLS + row * XW
                grid_ref[v * LH : (v + 1) * LH, column : column + XW] = pick_ref[
                    pl.ds(start, LH, stride=64), :
                ][:, :XW]
    for owner in range(2):
        points = grid_ref[:, owner * COLS : (owner + 1) * COLS].astype(jnp.bfloat16)
        columns = jnp.dot(points, stencil_ref[owner], preferred_element_type=jnp.float32)
        out_ref[owner : owner + 1, :] = jnp.sum(
            columns * level_ref[owner].astype(jnp.float32), axis=0, keepdims=True
        )


def observe(rows, lines, stencil, level):
    return pl.pallas_call(
        observe_kernel,
        out_shape=jax.ShapeDtypeStruct((2, REPORTS), jnp.float32),
        scratch_shapes=[
            pltpu.VMEM((LH * 64, 128), jnp.float32),
            pltpu.VMEM((NV * LH, 2 * COLS), jnp.float32),
        ],
        compiler_params=pltpu.CompilerParams(vmem_limit_bytes=48 * MIB),
        cost_estimate=pl.CostEstimate(
            flops=10**9, bytes_accessed=10 * MIB, transcendentals=0
        ),
        name="observe",
    )(rows, lines, stencil, level)


def spread_kernel(
    part_ref, peer_ref, mine_ref, other_ref, stencil_ref, level_ref, rows_ref,
    departure_ref, out_ref, pick_ref,
):
    for owner, ref in enumerate((mine_ref, other_ref)):
        value = part_ref[owner : owner + 1, :] + peer_ref[1 - owner : 2 - owner, :]
        departure = ref[11:12, :] * (value - ref[10:11, :])
        if owner == 0:
            departure_ref[...] = departure
        pushed = (level_ref[owner].astype(jnp.float32) * departure).astype(jnp.bfloat16)
        lifted = lax.dot_general(
            pushed, stencil_ref[owner], (((1,), (1,)), ((), ())), preferred_element_type=jnp.float32
        )
        lifted = jnp.concatenate([lifted, jnp.zeros((NV * LH, 128), jnp.float32)], axis=1)
        for v in range(NV):
            for row in range(ROWS):
                start = (owner * NV + v) * ROWS + row
                pick_ref[pl.ds(start, LH, stride=64), :] = lifted[
                    v * LH : (v + 1) * LH, row * XW : row * XW + 128
                ]
    parts = [pick_ref[level * 64 : (level + 1) * 64, :][:, :XW] for level in range(LH)]
    lines = jnp.concatenate(parts, axis=1).astype(jnp.bfloat16)
    out = jnp.dot(rows_ref[...], lines, preferred_element_type=jnp.float32)
    out_ref[...] = out.astype(jnp.bfloat16).reshape(NLAT, 16, LANES)


def spread(part, peer, mine, other, stencil, level, rows):
    return pl.pallas_call(
        spread_kernel,
        out_shape=[
            jax.ShapeDtypeStruct((1, REPORTS), jnp.float32),
            jax.ShapeDtypeStruct((NLAT, 16, LANES), jnp.bfloat16),
        ],
        scratch_shapes=[pltpu.VMEM((LH * 64, 128), jnp.float32)],
        compiler_params=pltpu.CompilerParams(vmem_limit_bytes=48 * MIB),
        cost_estimate=pl.CostEstimate(
            flops=10**9, bytes_accessed=10 * MIB, transcendentals=0
        ),
        name="spread",
    )(part, peer, mine, other, stencil, level, rows)


def on_device(
    control,
    zonal_scales,
    zonal_heights,
    meridional_scales,
    meridional_heights,
    vertical_map,
    send_blocks,
    report_slot,
    report_level,
    report_corner,
    report_weight,
    innovation,
    report_precision,
):
    strip = lax.axis_index("lat")
    half = lax.axis_index("obs")
    swap = [(0, 1), (1, 0)]

    mine = jnp.concatenate(
        [
            report_slot.reshape(1, -1).astype(jnp.float32),
            report_level.reshape(1, -1).astype(jnp.float32),
            report_corner.reshape(4, -1).astype(jnp.float32),
            report_weight.reshape(4, -1),
            innovation.reshape(1, -1),
            report_precision.reshape(1, -1),
        ],
        axis=0,
    )
    other = lax.ppermute(mine, "obs", swap)
    sends = send_blocks.reshape(2, 2)
    peer_sends = lax.ppermute(sends, "obs", swap)
    by_source = jnp.where(half == 0, jnp.stack([sends, peer_sends]), jnp.stack([peer_sends, sends]))
    by_owner = jnp.where(half == 0, by_source, by_source[:, ::-1]).transpose(1, 0, 2)
    anchor = jnp.arange(2).reshape(1, 2, 1, 1) * (NY // 2)
    rows = (anchor + by_owner[..., None] * 4 + jnp.arange(4)).reshape(2, 1, ROWS)
    rows = jnp.broadcast_to(rows, (2, NV, ROWS)).reshape(64)
    row_variable = (jnp.arange(64) // ROWS) % NV
    line = jnp.arange(NLAT * 16)
    line_row = (line // 16) * BAND + line % BAND
    line_variable = (line // BAND) % NV

    def meridional(a, av, b, bv):
        apart = jnp.abs(a - b).astype(jnp.float32)
        matrix = gaussians(apart, meridional_scales, meridional_heights)
        return jnp.where(av == bv, matrix, 0.0).astype(jnp.bfloat16)

    gather_rows = meridional(rows[:, None], row_variable[:, None], line_row[None], line_variable[None])
    spread_rows = meridional(line_row[:, None], line_variable[:, None], rows[None], row_variable[None])
    where = jnp.stack([strip % 8, half]).astype(jnp.int32)
    stencil, level = stencils(where, mine, other, vertical_map)

    smoothed, slab = forward_zonal(
        control.reshape(NV * LH * BAND, NX), zonal_scales, zonal_heights
    )
    lines = lax.all_to_all(smoothed, "lat", split_axis=0, concat_axis=0, tiled=True)
    part = observe(gather_rows, lines, stencil, level)
    peer = lax.ppermute(part, "obs", swap)
    departure, back = spread(part, peer, mine, other, stencil, level, spread_rows)
    back = lax.all_to_all(back, "lat", split_axis=0, concat_axis=0, tiled=True)
    gradient = backward_zonal(slab, back)
    return departure.reshape(report_slot.shape), gradient


def solution(mesh):
    in_specs = (
        P(None, "obs", "lat", None),
        P(),
        P(),
        P(),
        P(),
        P(),
        P("lat", "obs", None, None),
        P("lat", "obs", None),
        P("lat", "obs", None),
        P("lat", "obs", None, None),
        P("lat", "obs", None, None),
        P("lat", "obs", None),
        P("lat", "obs", None),
    )
    out_specs = (P("lat", "obs", None), P(None, "obs", "lat", None))
    return jax.shard_map(
        on_device, mesh=mesh, in_specs=in_specs, out_specs=out_specs, check_vma=False
    )
```

```python
import math

import jax
import jax.numpy as jnp
from jax import lax
from jax.experimental import pallas as pl
from jax.experimental.pallas import tpu as pltpu
from jax.sharding import PartitionSpec as P

NV = 2
LH = 32
NX = 3072
NY = 512
XW = 48
BAND = 8
NLAT = 64
GROUP = 8 * XW
LANES = LH * XW
TILE = 256
HALF = NX // 2
WIDE = 3 * TILE
EDGE = HALF - TILE
SLAB = EDGE + HALF
STEPS = HALF // WIDE
NARROW = 2 * TILE
ROWS = 16
COLS = ROWS * XW
REPORTS = 2048
SLOTS = 2
BR = 4
MIB = 2**20
LINES = NV * LH
VALUES = LINES + NV * ROWS
TABLE = VALUES + 16
FORWARD_MIB = 60
BACKWARD_MIB = 30
PREPARE_MIB = 16
OBSERVE_MIB = 45
SPREAD_MIB = 16

PIECES = (
    ((0, 48), (1, 96), (2, 128)),
    ((2, 16), (3, 64), (4, 112), (5, 128)),
    ((5, 32), (6, 80), (7, 128)),
)


def gaussians(distance, scales, heights):
    total = jnp.zeros(distance.shape, jnp.float32)
    for member in range(4):
        scale = scales[member]
        total = total + heights[member] * jnp.exp(
            -distance * distance / (2.0 * scale * scale)
        ) / jnp.sqrt(math.sqrt(math.pi) * scale)
    return total


def fill_slabs(scales_ref, heights_ref, slab_ref):
    shape = (8, NX)
    turn = lax.broadcasted_iota(jnp.int32, shape, 1) - HALF - lax.broadcasted_iota(
        jnp.int32, shape, 0
    )
    offset = jnp.abs(turn)
    distance = jnp.minimum(offset, NX - offset).astype(jnp.float32)
    scales = [scales_ref[0:1, m : m + 1] for m in range(4)]
    heights = [heights_ref[0:1, m : m + 1] for m in range(4)]
    near = gaussians(distance, scales, heights).astype(jnp.bfloat16).astype(jnp.float32)
    far = jnp.concatenate([near[:, HALF:], near[:, :HALF]], axis=1)
    for part, base in enumerate((0.5 * (near + far), 0.5 * (near - far))):
        for pair in range(TILE // 16):
            upper = base if pair == 0 else pltpu.roll(base, 16 * pair, 1)
            lower = pltpu.roll(base, 16 * pair + 8, 1)
            both = jnp.concatenate([upper, lower], axis=0)[:, TILE:]
            slab_ref[part, 16 * pair : 16 * pair + 16, :] = both.astype(jnp.bfloat16)


def zonal_columns(slab_ref, part, low, width):
    blocks = []
    for block in range(HALF // TILE):
        start = EDGE + low - TILE * block
        blocks.append(slab_ref[part, :, start : start + width])
    return jnp.concatenate(blocks, axis=0)


def zonal_halves(parts_ref, slab_ref, low, width):
    even, odd = [
        jnp.dot(
            parts_ref[part],
            zonal_columns(slab_ref, part, low, width),
            preferred_element_type=jnp.float32,
        )
        for part in range(2)
    ]
    return even + odd, even - odd


def pick(tiles, shift, lane):
    result = []
    for tile, pieces in enumerate(PIECES):
        low = 128 * tile
        value = tiles[(pieces[-1][0] - shift) % 8][:, low : low + 128]
        for block, end in pieces[-2::-1]:
            value = jnp.where(lane < end, tiles[(block - shift) % 8][:, low : low + 128], value)
        result.append(value)
    return jnp.concatenate(result, axis=1)


def forward_zonal_kernel(
    scales_hbm, heights_hbm, field_hbm, out_hbm,
    scales_ref, heights_ref, slab_ref, held_ref, parts_ref, acc_ref, out_ref, load_sems, store_sems,
):
    quarter = NV * LH * BAND // 4
    chunks = [pl.ds(quarter * k, quarter) for k in range(4)]
    loads = [
        pltpu.make_async_copy(source, target, load_sems.at[k])
        for k, (source, target) in enumerate(
            [(scales_hbm, scales_ref), (heights_hbm, heights_ref)]
            + [(field_hbm.at[chunk], held_ref.at[chunk]) for chunk in chunks]
        )
    ]
    for load in loads:
        load.start()
    loads[0].wait()
    loads[1].wait()
    fill_slabs(scales_ref, heights_ref, slab_ref)
    for k, chunk in enumerate(chunks):
        loads[2 + k].wait()
        west, east = held_ref[chunk, :HALF], held_ref[chunk, HALF:]
        parts_ref[0, chunk] = west + east
        parts_ref[1, chunk] = west - east
    lane = lax.broadcasted_iota(jnp.int32, (16, 128), 1)
    stores = []
    for step in range(STEPS):
        for side, value in enumerate(zonal_halves(parts_ref, slab_ref, WIDE * step, WIDE)):
            acc_ref[step, side] = value
        for side in range(2):
            for strips in range(2):
                first = side * (NLAT // 2) + step * 16 + strips * 8
                for group in range(LH // 8):
                    turned = []
                    for j in range(8):
                        row = (group * 8 + j) * BAND
                        both = jnp.concatenate(
                            [
                                acc_ref[step, side, v * LH * BAND + row : v * LH * BAND + row + BAND,
                                        strips * GROUP : (strips + 1) * GROUP]
                                for v in range(NV)
                            ],
                            axis=0,
                        )
                        turned.append(both if j == 0 else pltpu.roll(both, XW * j, 1))
                    for i in range(8):
                        out_ref[first + i, :, group * GROUP : (group + 1) * GROUP] = pick(
                            turned, i, lane
                        ).astype(jnp.bfloat16)
                store = pltpu.make_async_copy(
                    out_ref.at[first : first + 8], out_hbm.at[first : first + 8], store_sems.at[first // 8]
                )
                store.start()
                stores.append(store)
    for store in stores:
        store.wait()


def forward_zonal(field, scales, heights):
    rows = NV * LH * BAND
    hbm = pl.BlockSpec(memory_space=pltpu.HBM)
    return pl.pallas_call(
        forward_zonal_kernel,
        in_specs=[hbm] * 3,
        out_specs=hbm,
        out_shape=jax.ShapeDtypeStruct((NLAT, 16, LANES), jnp.bfloat16),
        scratch_shapes=[
            pltpu.VMEM((1, 4), jnp.float32),
            pltpu.VMEM((1, 4), jnp.float32),
            pltpu.VMEM((2, TILE, SLAB), jnp.bfloat16),
            pltpu.VMEM((rows, NX), jnp.bfloat16),
            pltpu.VMEM((2, rows, HALF), jnp.bfloat16),
            pltpu.VMEM((STEPS, 2, rows, WIDE), jnp.float32),
            pltpu.VMEM((NLAT, 16, LANES), jnp.bfloat16),
            pltpu.SemaphoreType.DMA((6,)),
            pltpu.SemaphoreType.DMA((NLAT // 8,)),
        ],
        compiler_params=pltpu.CompilerParams(vmem_limit_bytes=FORWARD_MIB * MIB),
        cost_estimate=pl.CostEstimate(
            flops=rows * NX * NX, bytes_accessed=8 * MIB, transcendentals=10**5
        ),
        name="forward_zonal",
    )(scales.reshape(1, 4), heights.reshape(1, 4), field)


def backward_zonal_kernel(
    slab_hbm, lines_ref, out_hbm, slab_ref, parts_ref, acc_ref, load_sem, sems
):
    load = pltpu.make_async_copy(slab_hbm, slab_ref, load_sem)
    load.start()
    lane = lax.broadcasted_iota(jnp.int32, (16, 128), 1)

    def levels(strips, group):
        tiles = [
            lines_ref[strips * 8 + i, :, group * GROUP : (group + 1) * GROUP].astype(jnp.float32)
            for i in range(8)
        ]
        picked = [pick(tiles, j, lane) for j in range(8)]
        return [p if j == 0 else pltpu.roll(p, GROUP - XW * j, 1) for j, p in enumerate(picked)]

    def fill(strips, carry):
        start = pl.multiple_of(strips * GROUP, 128)
        for group in range(LH // 8):
            west = levels(strips, group)
            east = levels(strips + NLAT // 16, group)
            for j in range(8):
                row = (group * 8 + j) * 16
                for part, value in enumerate((west[j] + east[j], west[j] - east[j])):
                    parts_ref[part, row : row + 16, pl.ds(start, GROUP)] = value.astype(
                        jnp.bfloat16
                    )
        return carry

    lax.fori_loop(0, NLAT // 16, fill, 0)
    load.wait()
    stores = []
    for step in range(HALF // NARROW):
        for side, value in enumerate(zonal_halves(parts_ref, slab_ref, NARROW * step, NARROW)):
            for level in range(LH):
                for v in range(NV):
                    row = (level * NV + v) * BAND
                    acc_ref[step, side, v, level] = value[row : row + BAND]
        for side in range(2):
            low = side * HALF + step * NARROW
            store = pltpu.make_async_copy(
                acc_ref.at[step, side], out_hbm.at[:, :, :, low : low + NARROW], sems.at[step, side]
            )
            store.start()
            stores.append(store)
    for store in stores:
        store.wait()


def backward_zonal(slab, lines):
    rows = NV * LH * BAND
    hbm = pl.BlockSpec(memory_space=pltpu.HBM)
    return pl.pallas_call(
        backward_zonal_kernel,
        in_specs=[hbm, pl.BlockSpec(memory_space=pltpu.VMEM)],
        out_specs=hbm,
        out_shape=jax.ShapeDtypeStruct((NV, LH, BAND, NX), jnp.float32),
        scratch_shapes=[
            pltpu.VMEM((2, TILE, SLAB), jnp.bfloat16),
            pltpu.VMEM((2, rows, HALF), jnp.bfloat16),
            pltpu.VMEM((HALF // NARROW, 2, NV, LH, BAND, NARROW), jnp.float32),
            pltpu.SemaphoreType.DMA,
            pltpu.SemaphoreType.DMA((HALF // NARROW, 2)),
        ],
        compiler_params=pltpu.CompilerParams(vmem_limit_bytes=BACKWARD_MIB * MIB),
        cost_estimate=pl.CostEstimate(
            flops=rows * NX * NX, bytes_accessed=12 * MIB, transcendentals=0
        ),
        name="backward_zonal",
    )(slab, lines)


def fill_stencil(table_ref, owner, stencil_ref):
    chunk = 256
    for low in range(0, REPORTS, chunk):
        part = slice(low, low + chunk)
        values = table_ref[owner, VALUES:TABLE, part].astype(jnp.float32)
        corner = values[1:2].astype(jnp.int32)
        first = values[0:1].astype(jnp.int32) * BR + corner // XW
        cell = lax.rem(corner, XW)
        column = lax.broadcasted_iota(jnp.int32, (XW, chunk), 0)
        west, east = column == cell, column == cell + 1
        lower, upper = [
            jnp.where(west, values[c : c + 1], jnp.where(east, values[c + 1 : c + 2], 0.0))
            for c in (2, 4)
        ]
        for row in range(ROWS):
            value = jnp.where(first == row, lower, jnp.where(first == row - 1, upper, 0.0))
            stencil_ref[owner, row * XW : (row + 1) * XW, part] = value.astype(jnp.bfloat16)


def prepare_kernel(
    where_ref, sends_ref, peer_sends_ref, zonal_scales_ref, zonal_heights_ref, scales_ref, heights_ref,
    mine_ref, other_ref, map_ref, table_ref, spread_ref, slab_ref,
):
    fill_slabs(zonal_scales_ref, zonal_heights_ref, slab_ref)
    strip_turn, half = where_ref[0], where_ref[1]
    shape = (LH, 2 * LH)
    slot = lax.broadcasted_iota(jnp.int32, shape, 0)
    level = (slot // 8) * 8 + lax.rem(lax.rem(slot, 8) + (8 - strip_turn), 8) + LH * half
    order = (lax.broadcasted_iota(jnp.int32, shape, 1) == level).astype(jnp.bfloat16)
    row = lax.broadcasted_iota(jnp.int32, (64, 128), 0)
    place = lax.rem(row, 4)
    for owner in range(2):
        target = half if owner == 0 else 1 - half
        for source in range(2):
            for turn in range(SLOTS):
                block = jnp.where(
                    half == source, sends_ref[target, turn], peer_sends_ref[target, turn]
                )
                chosen = (row // 32 == owner) & (
                    lax.rem(row // 4, 4) == source * SLOTS + turn
                )
                place = place + jnp.where(chosen, source * (NY // 2) + block * 4, 0)
    line = lax.broadcasted_iota(jnp.int32, (64, NLAT * 16), 1)
    apart = jnp.abs(place[:, :1] - ((line // 16) * BAND + lax.rem(line, BAND))).astype(jnp.float32)
    matrix = gaussians(
        apart,
        [scales_ref[0:1, m : m + 1] for m in range(4)],
        [heights_ref[0:1, m : m + 1] for m in range(4)],
    )
    own = lax.rem(row // ROWS, NV)[:, :1] == lax.rem(line // BAND, NV)
    matrix = jnp.where(own, matrix, 0.0)
    spread_ref[...] = matrix.T.astype(jnp.bfloat16)
    matrix = matrix.astype(jnp.bfloat16)
    blank = jnp.zeros((NV * ROWS, REPORTS - NLAT * 16), jnp.bfloat16)
    for owner in range(2):
        table_ref[owner, LINES:VALUES, : NLAT * 16] = matrix[owner * 32 : (owner + 1) * 32]
        table_ref[owner, LINES:VALUES, NLAT * 16 :] = blank
    for owner, ref in enumerate((mine_ref, other_ref)):
        code = ref[1:2, :].astype(jnp.int32)
        for v in range(NV):
            rows = lax.broadcasted_iota(jnp.int32, (2 * LH, REPORTS), 0) + 2 * LH * v
            hot = (rows == code).astype(jnp.float32).astype(jnp.bfloat16)
            picked = lax.dot_general(
                map_ref[v], hot, (((0,), (0,)), ((), ())), preferred_element_type=jnp.float32
            ).astype(jnp.bfloat16)
            table_ref[owner, v * LH : (v + 1) * LH, :] = jnp.dot(
                order, picked, preferred_element_type=jnp.float32
            ).astype(jnp.bfloat16)
        values = [ref[0:1, :], ref[2:3, :], ref[6:10, :]]
        for row in (10, 11):
            rest = ref[row : row + 1, :]
            for _ in range(3):
                term = rest.astype(jnp.bfloat16).astype(jnp.float32)
                values.append(term)
                rest = rest - term
        values.append(jnp.zeros((4, REPORTS), jnp.float32))
        table_ref[owner, VALUES:TABLE, :] = jnp.concatenate(values, axis=0).astype(jnp.bfloat16)


def prepare(where, sends, peer_sends, zonal, meridional, mine, other, vertical_map):
    smem = pl.BlockSpec(memory_space=pltpu.SMEM)
    vmem = pl.BlockSpec(memory_space=pltpu.VMEM)
    return pl.pallas_call(
        prepare_kernel,
        in_specs=[smem] * 3 + [vmem] * 7,
        out_shape=[
            jax.ShapeDtypeStruct((2, TABLE, REPORTS), jnp.bfloat16),
            jax.ShapeDtypeStruct((NLAT * 16, 64), jnp.bfloat16),
            jax.ShapeDtypeStruct((2, TILE, SLAB), jnp.bfloat16),
        ],
        compiler_params=pltpu.CompilerParams(vmem_limit_bytes=PREPARE_MIB * MIB),
        cost_estimate=pl.CostEstimate(
            flops=10**9, bytes_accessed=8 * MIB, transcendentals=3 * 10**5
        ),
        name="prepare",
    )(where, sends, peer_sends, *[x.reshape(1, 4) for x in zonal + meridional], mine, other, vertical_map)


def observe_kernel(
    table_hbm, rows_hbm, lines_ref, out_ref, stencil_ref, table_ref, rows_ref, pick_ref, grid_ref, sems
):
    loads = [
        pltpu.make_async_copy(table_hbm, table_ref, sems.at[0]),
        pltpu.make_async_copy(rows_hbm, rows_ref, sems.at[1]),
    ]
    for load in loads:
        load.start()
    loads[0].wait()
    rows = jnp.concatenate([table_ref[o, LINES:VALUES, : NLAT * 16] for o in range(2)], axis=0)
    lines = lines_ref[...].reshape(NLAT * 16, LANES)
    mixed = jnp.dot(rows, lines, preferred_element_type=jnp.float32)
    mixed = mixed.astype(jnp.bfloat16).astype(jnp.float32)
    for level in range(LH):
        pick_ref[level * 64 : (level + 1) * 64, :XW] = mixed[:, level * XW : (level + 1) * XW]
    for owner in range(2):
        for v in range(NV):
            for row in range(ROWS):
                start = (owner * NV + v) * ROWS + row
                column = owner * COLS + row * XW
                grid_ref[v * LH : (v + 1) * LH, column : column + XW] = pick_ref[
                    pl.ds(start, LH, stride=64), :
                ][:, :XW]
    for owner in range(2):
        fill_stencil(table_ref, owner, stencil_ref)
        points = grid_ref[:, owner * COLS : (owner + 1) * COLS].astype(jnp.bfloat16)
        columns = jnp.dot(points, stencil_ref[owner], preferred_element_type=jnp.float32)
        out_ref[owner : owner + 1, :] = jnp.sum(
            columns * table_ref[owner, :LINES, :].astype(jnp.float32), axis=0, keepdims=True
        )
    loads[1].wait()


def observe(table, rows, lines):
    hbm = pl.BlockSpec(memory_space=pltpu.HBM)
    vmem = pl.BlockSpec(memory_space=pltpu.VMEM)
    return pl.pallas_call(
        observe_kernel,
        in_specs=[hbm, hbm, vmem],
        out_specs=[vmem] * 4,
        out_shape=[
            pltpu.VMEM((2, REPORTS), jnp.float32),
            pltpu.VMEM((2, COLS, REPORTS), jnp.bfloat16),
            pltpu.VMEM(table.shape, jnp.bfloat16),
            pltpu.VMEM(rows.shape, jnp.bfloat16),
        ],
        scratch_shapes=[
            pltpu.VMEM((LH * 64, 128), jnp.float32),
            pltpu.VMEM((NV * LH, 2 * COLS), jnp.float32),
            pltpu.SemaphoreType.DMA((2,)),
        ],
        compiler_params=pltpu.CompilerParams(vmem_limit_bytes=OBSERVE_MIB * MIB),
        cost_estimate=pl.CostEstimate(
            flops=10**9, bytes_accessed=10 * MIB, transcendentals=0
        ),
        name="observe",
    )(table, rows, lines)


def spread_kernel(part_ref, peer_ref, stencil_ref, table_ref, rows_ref, departure_ref, out_ref, pick_ref):
    for owner in range(2):
        value = part_ref[owner : owner + 1, :] + peer_ref[1 - owner : 2 - owner, :]
        terms = table_ref[owner, VALUES:TABLE, :].astype(jnp.float32)
        innovation, precision = [
            terms[k : k + 1] + terms[k + 1 : k + 2] + terms[k + 2 : k + 3] for k in (6, 9)
        ]
        departure = precision * (value - innovation)
        if owner == 0:
            departure_ref[...] = departure
        level = table_ref[owner, :LINES, :].astype(jnp.float32)
        pushed = (level * departure).astype(jnp.bfloat16)
        lifted = lax.dot_general(
            pushed,
            stencil_ref[owner],
            (((1,), (1,)), ((), ())),
            preferred_element_type=jnp.float32,
        )
        lifted = jnp.concatenate([lifted, jnp.zeros((NV * LH, 128), jnp.float32)], axis=1)
        for v in range(NV):
            for row in range(ROWS):
                start = (owner * NV + v) * ROWS + row
                pick_ref[pl.ds(start, LH, stride=64), :] = lifted[
                    v * LH : (v + 1) * LH, row * XW : row * XW + 128
                ]
    parts = [pick_ref[level * 64 : (level + 1) * 64, :][:, :XW] for level in range(LH)]
    lines = jnp.concatenate(parts, axis=1).astype(jnp.bfloat16)
    out = jnp.dot(rows_ref[...], lines, preferred_element_type=jnp.float32)
    out_ref[...] = out.astype(jnp.bfloat16).reshape(NLAT, 16, LANES)


def spread(part, peer, held):
    vmem = pl.BlockSpec(memory_space=pltpu.VMEM)
    return pl.pallas_call(
        spread_kernel,
        in_specs=[vmem] * 5,
        out_shape=[
            jax.ShapeDtypeStruct((1, REPORTS), jnp.float32),
            jax.ShapeDtypeStruct((NLAT, 16, LANES), jnp.bfloat16),
        ],
        scratch_shapes=[pltpu.VMEM((LH * 64, 128), jnp.float32)],
        compiler_params=pltpu.CompilerParams(vmem_limit_bytes=SPREAD_MIB * MIB),
        cost_estimate=pl.CostEstimate(
            flops=10**9, bytes_accessed=10 * MIB, transcendentals=0
        ),
        name="spread",
    )(part, peer, *held)


def on_device(
    control,
    zonal_scales,
    zonal_heights,
    meridional_scales,
    meridional_heights,
    vertical_map,
    send_blocks,
    report_slot,
    report_level,
    report_corner,
    report_weight,
    innovation,
    report_precision,
):
    strip = lax.axis_index("lat")
    half = lax.axis_index("obs")
    swap = [(0, 1), (1, 0)]

    mine = jnp.concatenate(
        [
            report_slot.reshape(1, -1).astype(jnp.float32),
            report_level.reshape(1, -1).astype(jnp.float32),
            report_corner.reshape(4, -1).astype(jnp.float32),
            report_weight.reshape(4, -1),
            innovation.reshape(1, -1),
            report_precision.reshape(1, -1),
        ],
        axis=0,
    )
    other = lax.ppermute(mine, "obs", swap)
    sends = send_blocks.reshape(2, 2)
    peer_sends = lax.ppermute(sends, "obs", swap)
    where = jnp.stack([strip % 8, half]).astype(jnp.int32)
    table, spread_rows, slab = prepare(
        where,
        sends,
        peer_sends,
        (zonal_scales, zonal_heights),
        (meridional_scales, meridional_heights),
        mine,
        other,
        vertical_map,
    )

    smoothed = forward_zonal(control.reshape(NV * LH * BAND, NX), zonal_scales, zonal_heights)
    lines = lax.all_to_all(smoothed, "lat", split_axis=0, concat_axis=0, tiled=True)
    part, *held = observe(table, spread_rows, lines)
    peer = lax.ppermute(part, "obs", swap)
    departure, back = spread(part, peer, held)
    back = lax.all_to_all(back, "lat", split_axis=0, concat_axis=0, tiled=True)
    gradient = backward_zonal(slab, back)
    return departure.reshape(report_slot.shape), gradient


def solution(mesh):
    in_specs = (
        P(None, "obs", "lat", None),
        P(),
        P(),
        P(),
        P(),
        P(),
        P("lat", "obs", None, None),
        P("lat", "obs", None),
        P("lat", "obs", None),
        P("lat", "obs", None, None),
        P("lat", "obs", None, None),
        P("lat", "obs", None),
        P("lat", "obs", None),
    )
    out_specs = (P("lat", "obs", None), P(None, "obs", "lat", None))
    return jax.shard_map(
        on_device, mesh=mesh, in_specs=in_specs, out_specs=out_specs, check_vma=False
    )
```

```python
import math

import jax
import jax.numpy as jnp
from jax import lax
from jax.experimental import pallas as pl
from jax.experimental.pallas import tpu as pltpu
from jax.sharding import PartitionSpec as P

NV = 2
LH = 32
NX = 3072
NY = 512
XW = 48
BAND = 8
NLAT = 64
GROUP = 8 * XW
LANES = LH * XW
TILE = 256
HALF = NX // 2
QUARTER = NX // 4
SLAB_SUM = 2 * HALF - TILE
SLAB_DIFFERENCE = SLAB_SUM + 2 * QUARTER - TILE
SLAB = SLAB_DIFFERENCE + 2 * QUARTER - TILE
ROWS = 16
COLS = ROWS * XW
REPORTS = 2048
SLOTS = 2
BR = 4
MIB = 2**20
LINES = NV * LH
VALUES = LINES + NV * ROWS
TABLE = VALUES + 16
FORWARD_MIB = 60
BACKWARD_MIB = 30
PREPARE_MIB = 16
OBSERVE_MIB = 45
SPREAD_MIB = 16

PIECES = (
    ((0, 48), (1, 96), (2, 128)),
    ((2, 16), (3, 64), (4, 112), (5, 128)),
    ((5, 32), (6, 80), (7, 128)),
)


def gaussians(distance, scales, heights):
    total = jnp.zeros(distance.shape, jnp.float32)
    for member in range(4):
        scale = scales[member]
        total = total + heights[member] * jnp.exp(
            -distance * distance / (2.0 * scale * scale)
        ) / jnp.sqrt(math.sqrt(math.pi) * scale)
    return total


def fill_slabs(scales_ref, heights_ref, slab_ref):
    shape = (8, NX)
    turn = lax.broadcasted_iota(jnp.int32, shape, 1) - HALF - lax.broadcasted_iota(
        jnp.int32, shape, 0
    )
    offset = jnp.abs(turn)
    distance = jnp.minimum(offset, NX - offset).astype(jnp.float32)
    scales = [scales_ref[0:1, m : m + 1] for m in range(4)]
    heights = [heights_ref[0:1, m : m + 1] for m in range(4)]
    near = gaussians(distance, scales, heights).astype(jnp.bfloat16).astype(jnp.float32)
    far = jnp.concatenate([near[:, HALF:], near[:, :HALF]], axis=1)
    total = near + far
    shifted = jnp.concatenate([total[:, QUARTER:], total[:, :QUARTER]], axis=1)
    for base, low, high, length in (
        (0.5 * (near - far), 0, SLAB_SUM, HALF),
        (0.25 * (total + shifted), SLAB_SUM, SLAB_DIFFERENCE, QUARTER),
        (0.25 * (total - shifted), SLAB_DIFFERENCE, SLAB, QUARTER),
    ):
        first = HALF - length + TILE
        for pair in range(TILE // 16):
            upper = base if pair == 0 else pltpu.roll(base, 16 * pair, 1)
            lower = pltpu.roll(base, 16 * pair + 8, 1)
            both = jnp.concatenate([upper, lower], axis=0)[:, first : first + high - low]
            slab_ref[16 * pair : 16 * pair + 16, low:high] = both.astype(jnp.bfloat16)


def zonal_part(parts_ref, slab_ref, first, start, length, low, width):
    blocks = []
    for block in range(length // TILE):
        left = start + length - TILE + low - TILE * block
        blocks.append(slab_ref[:, left : left + width])
    return jnp.dot(
        parts_ref[:, first : first + length],
        jnp.concatenate(blocks, axis=0),
        preferred_element_type=jnp.float32,
    )


def zonal_quarters(parts_ref, slab_ref, low, width):
    total = zonal_part(parts_ref, slab_ref, HALF, SLAB_SUM, QUARTER, low, width)
    change = zonal_part(
        parts_ref, slab_ref, HALF + QUARTER, SLAB_DIFFERENCE, QUARTER, low, width
    )
    west = zonal_part(parts_ref, slab_ref, 0, 0, HALF, low, width)
    east = zonal_part(parts_ref, slab_ref, 0, 0, HALF, QUARTER + low, width)
    first, second = total + change, total - change
    return first + west, second + east, first - west, second - east


def zonal_split(quarters):
    first, second = quarters[0] + quarters[2], quarters[1] + quarters[3]
    pieces = (quarters[0] - quarters[2], quarters[1] - quarters[3], first + second, first - second)
    return [piece.astype(jnp.bfloat16) for piece in pieces]


def pick(tiles, shift, lane):
    result = []
    for tile, pieces in enumerate(PIECES):
        low = 128 * tile
        value = tiles[(pieces[-1][0] - shift) % 8][:, low : low + 128]
        for block, end in pieces[-2::-1]:
            value = jnp.where(lane < end, tiles[(block - shift) % 8][:, low : low + 128], value)
        result.append(value)
    return jnp.concatenate(result, axis=1)


def forward_zonal_kernel(
    scales_hbm, heights_hbm, field_hbm, out_hbm,
    scales_ref, heights_ref, slab_ref, held_ref, parts_ref, acc_ref, out_ref, load_sems, store_sems,
):
    quarter = NV * LH * BAND // 4
    chunks = [pl.ds(quarter * k, quarter) for k in range(4)]
    loads = [
        pltpu.make_async_copy(source, target, load_sems.at[k])
        for k, (source, target) in enumerate(
            [(scales_hbm, scales_ref), (heights_hbm, heights_ref)]
            + [(field_hbm.at[chunk], held_ref.at[chunk]) for chunk in chunks]
        )
    ]
    for load in loads:
        load.start()
    loads[0].wait()
    loads[1].wait()
    fill_slabs(scales_ref, heights_ref, slab_ref)
    for k, chunk in enumerate(chunks):
        loads[2 + k].wait()
        quarters = [
            held_ref[chunk, QUARTER * q : QUARTER * (q + 1)].astype(jnp.float32) for q in range(4)
        ]
        for q, piece in enumerate(zonal_split(quarters)):
            parts_ref[chunk, QUARTER * q : QUARTER * (q + 1)] = piece
    lane = lax.broadcasted_iota(jnp.int32, (16, 128), 1)
    stores = []
    for q, value in enumerate(zonal_quarters(parts_ref, slab_ref, 0, QUARTER)):
        acc_ref[q] = value
    for q in range(4):
        for strips in range(2):
            first = q * 16 + strips * 8
            for group in range(LH // 8):
                turned = []
                for j in range(8):
                    row = (group * 8 + j) * BAND
                    both = jnp.concatenate(
                        [
                            acc_ref[q, v * LH * BAND + row : v * LH * BAND + row + BAND,
                                    strips * GROUP : (strips + 1) * GROUP]
                            for v in range(NV)
                        ],
                        axis=0,
                    )
                    both = both if j == 0 else pltpu.roll(both, XW * j, 1)
                    turned.append(both.astype(jnp.bfloat16))
                for i in range(8):
                    out_ref[first + i, :, group * GROUP : (group + 1) * GROUP] = pick(
                        turned, i, lane
                    )
            store = pltpu.make_async_copy(
                out_ref.at[first : first + 8], out_hbm.at[first : first + 8], store_sems.at[first // 8]
            )
            store.start()
            stores.append(store)
    for store in stores:
        store.wait()


def forward_zonal(field, scales, heights):
    rows = NV * LH * BAND
    hbm = pl.BlockSpec(memory_space=pltpu.HBM)
    return pl.pallas_call(
        forward_zonal_kernel,
        in_specs=[hbm] * 3,
        out_specs=hbm,
        out_shape=jax.ShapeDtypeStruct((NLAT, 16, LANES), jnp.bfloat16),
        scratch_shapes=[
            pltpu.VMEM((1, 4), jnp.float32),
            pltpu.VMEM((1, 4), jnp.float32),
            pltpu.VMEM((TILE, SLAB), jnp.bfloat16),
            pltpu.VMEM((rows, NX), jnp.bfloat16),
            pltpu.VMEM((rows, NX), jnp.bfloat16),
            pltpu.VMEM((4, rows, QUARTER), jnp.float32),
            pltpu.VMEM((NLAT, 16, LANES), jnp.bfloat16),
            pltpu.SemaphoreType.DMA((6,)),
            pltpu.SemaphoreType.DMA((NLAT // 8,)),
        ],
        compiler_params=pltpu.CompilerParams(vmem_limit_bytes=FORWARD_MIB * MIB),
        cost_estimate=pl.CostEstimate(
            flops=rows * NX * NX, bytes_accessed=8 * MIB, transcendentals=10**5
        ),
        name="forward_zonal",
    )(scales.reshape(1, 4), heights.reshape(1, 4), field)


def backward_zonal_kernel(
    slab_hbm, lines_ref, out_hbm, slab_ref, parts_ref, acc_ref, load_sem, sems
):
    load = pltpu.make_async_copy(slab_hbm, slab_ref, load_sem)
    load.start()
    lane = lax.broadcasted_iota(jnp.int32, (16, 128), 1)

    def levels(strips, group):
        tiles = [
            lines_ref[strips * 8 + i, :, group * GROUP : (group + 1) * GROUP] for i in range(8)
        ]
        picked = [pick(tiles, j, lane).astype(jnp.float32) for j in range(8)]
        return [p if j == 0 else pltpu.roll(p, GROUP - XW * j, 1) for j, p in enumerate(picked)]

    def fill(strips, carry):
        for group in range(LH // 8):
            quarters = [levels(strips + NLAT // 32 * q, group) for q in range(4)]
            for j in range(8):
                row = (group * 8 + j) * 16
                for q, piece in enumerate(zonal_split([quarter[j] for quarter in quarters])):
                    start = pl.multiple_of(strips * GROUP + q * QUARTER, 128)
                    parts_ref[row : row + 16, pl.ds(start, GROUP)] = piece
        return carry

    lax.fori_loop(0, NLAT // 32, fill, 0)
    load.wait()
    stores = []
    for step in range(QUARTER // TILE):
        low = step * TILE
        for q, value in enumerate(zonal_quarters(parts_ref, slab_ref, low, TILE)):
            for level in range(LH):
                for v in range(NV):
                    row = (level * NV + v) * BAND
                    acc_ref[step, q, v, level] = value[row : row + BAND]
        for q in range(4):
            left = q * QUARTER + low
            store = pltpu.make_async_copy(
                acc_ref.at[step, q], out_hbm.at[:, :, :, left : left + TILE], sems.at[step, q]
            )
            store.start()
            stores.append(store)
    for store in stores:
        store.wait()


def backward_zonal(slab, lines):
    rows = NV * LH * BAND
    hbm = pl.BlockSpec(memory_space=pltpu.HBM)
    return pl.pallas_call(
        backward_zonal_kernel,
        in_specs=[hbm, pl.BlockSpec(memory_space=pltpu.VMEM)],
        out_specs=hbm,
        out_shape=jax.ShapeDtypeStruct((NV, LH, BAND, NX), jnp.float32),
        scratch_shapes=[
            pltpu.VMEM((TILE, SLAB), jnp.bfloat16),
            pltpu.VMEM((rows, NX), jnp.bfloat16),
            pltpu.VMEM((QUARTER // TILE, 4, NV, LH, BAND, TILE), jnp.float32),
            pltpu.SemaphoreType.DMA,
            pltpu.SemaphoreType.DMA((QUARTER // TILE, 4)),
        ],
        compiler_params=pltpu.CompilerParams(vmem_limit_bytes=BACKWARD_MIB * MIB),
        cost_estimate=pl.CostEstimate(
            flops=rows * NX * NX, bytes_accessed=12 * MIB, transcendentals=0
        ),
        name="backward_zonal",
    )(slab, lines)


def fill_stencil(table_ref, owner, stencil_ref):
    chunk = 256
    for low in range(0, REPORTS, chunk):
        part = slice(low, low + chunk)
        values = table_ref[owner, VALUES:TABLE, part].astype(jnp.float32)
        corner = values[1:2].astype(jnp.int32)
        first = values[0:1].astype(jnp.int32) * BR + corner // XW
        cell = lax.rem(corner, XW)
        column = lax.broadcasted_iota(jnp.int32, (XW, chunk), 0)
        west, east = column == cell, column == cell + 1
        lower, upper = [
            jnp.where(west, values[c : c + 1], jnp.where(east, values[c + 1 : c + 2], 0.0))
            for c in (2, 4)
        ]
        for row in range(ROWS):
            value = jnp.where(first == row, lower, jnp.where(first == row - 1, upper, 0.0))
            stencil_ref[owner, row * XW : (row + 1) * XW, part] = value.astype(jnp.bfloat16)


def prepare_kernel(
    where_ref, sends_ref, peer_sends_ref, zonal_scales_ref, zonal_heights_ref, scales_ref, heights_ref,
    mine_ref, other_ref, map_ref, table_ref, spread_ref, slab_ref, turned_ref, column_ref,
):
    fill_slabs(zonal_scales_ref, zonal_heights_ref, slab_ref)
    strip_turn, half = where_ref[0], where_ref[1]
    shape = (LH, 2 * LH)
    slot = lax.broadcasted_iota(jnp.int32, shape, 0)
    level = (slot // 8) * 8 + lax.rem(lax.rem(slot, 8) + (8 - strip_turn), 8) + LH * half
    order = (lax.broadcasted_iota(jnp.int32, shape, 1) == level).astype(jnp.bfloat16)
    row = lax.broadcasted_iota(jnp.int32, (64, 128), 0)
    place = lax.rem(row, 4)
    for owner in range(2):
        target = half if owner == 0 else 1 - half
        for source in range(2):
            for turn in range(SLOTS):
                block = jnp.where(
                    half == source, sends_ref[target, turn], peer_sends_ref[target, turn]
                )
                chosen = (row // 32 == owner) & (
                    lax.rem(row // 4, 4) == source * SLOTS + turn
                )
                place = place + jnp.where(chosen, source * (NY // 2) + block * 4, 0)
    line = lax.broadcasted_iota(jnp.int32, (64, NLAT * 16), 1)
    apart = jnp.abs(place[:, :1] - ((line // 16) * BAND + lax.rem(line, BAND))).astype(jnp.float32)
    matrix = gaussians(
        apart,
        [scales_ref[0:1, m : m + 1] for m in range(4)],
        [heights_ref[0:1, m : m + 1] for m in range(4)],
    )
    own = lax.rem(row // ROWS, NV)[:, :1] == lax.rem(line // BAND, NV)
    matrix = jnp.where(own, matrix, 0.0)
    spread_ref[...] = matrix.T.astype(jnp.bfloat16)
    matrix = matrix.astype(jnp.bfloat16)
    blank = jnp.zeros((NV * ROWS, REPORTS - NLAT * 16), jnp.bfloat16)
    for owner in range(2):
        table_ref[owner, LINES:VALUES, : NLAT * 16] = matrix[owner * 32 : (owner + 1) * 32]
        table_ref[owner, LINES:VALUES, NLAT * 16 :] = blank
    for owner, ref in enumerate((mine_ref, other_ref)):
        code = ref[1:2, :].astype(jnp.int32)
        for v in range(NV):
            rows = lax.broadcasted_iota(jnp.int32, (2 * LH, REPORTS), 0) + 2 * LH * v
            hot = (rows == code).astype(jnp.float32).astype(jnp.bfloat16)
            picked = lax.dot_general(
                map_ref[v], hot, (((0,), (0,)), ((), ())), preferred_element_type=jnp.float32
            ).astype(jnp.bfloat16)
            table_ref[owner, v * LH : (v + 1) * LH, :] = jnp.dot(
                order, picked, preferred_element_type=jnp.float32
            ).astype(jnp.bfloat16)
        values = [ref[0:1, :], ref[2:3, :], ref[6:10, :]]
        for row in (10, 11):
            rest = ref[row : row + 1, :]
            for _ in range(3):
                term = rest.astype(jnp.bfloat16).astype(jnp.float32)
                values.append(term)
                rest = rest - term
        values.append(jnp.zeros((4, REPORTS), jnp.float32))
        values = jnp.concatenate(values, axis=0)
        table_ref[owner, VALUES:TABLE, :] = values.astype(jnp.bfloat16)
        column_ref[...] = values.T

        def turn_stencil(step, carry):
            start = pl.multiple_of(step * 128, 128)
            columns = column_ref[pl.ds(start, 128), :]
            point = (columns[:, 0:1] * float(BR * XW) + columns[:, 1:2]).astype(jnp.int32)
            apart = lax.broadcasted_iota(jnp.int32, (128, COLS), 1) - point
            value = jnp.zeros((128, COLS), jnp.float32)
            for c, offset in enumerate((0, 1, XW, XW + 1)):
                value = jnp.where(apart == offset, columns[:, 2 + c : 3 + c], value)
            turned_ref[owner, pl.ds(start, 128), :] = value.astype(jnp.bfloat16)
            return carry

        lax.fori_loop(0, REPORTS // 128, turn_stencil, 0)


def prepare(where, sends, peer_sends, zonal, meridional, mine, other, vertical_map):
    smem = pl.BlockSpec(memory_space=pltpu.SMEM)
    vmem = pl.BlockSpec(memory_space=pltpu.VMEM)
    return pl.pallas_call(
        prepare_kernel,
        in_specs=[smem] * 3 + [vmem] * 7,
        out_shape=[
            jax.ShapeDtypeStruct((2, TABLE, REPORTS), jnp.bfloat16),
            jax.ShapeDtypeStruct((NLAT * 16, 64), jnp.bfloat16),
            jax.ShapeDtypeStruct((TILE, SLAB), jnp.bfloat16),
            jax.ShapeDtypeStruct((2, REPORTS, COLS), jnp.bfloat16),
        ],
        scratch_shapes=[pltpu.VMEM((REPORTS, 16), jnp.float32)],
        compiler_params=pltpu.CompilerParams(vmem_limit_bytes=PREPARE_MIB * MIB),
        cost_estimate=pl.CostEstimate(
            flops=10**9, bytes_accessed=8 * MIB, transcendentals=3 * 10**5
        ),
        name="prepare",
    )(where, sends, peer_sends, *[x.reshape(1, 4) for x in zonal + meridional], mine, other, vertical_map)


def observe_kernel(
    table_hbm, rows_hbm, turned_hbm, lines_ref, out_ref, table_ref, rows_ref, turned_ref,
    stencil_ref, pick_ref, grid_ref, sems,
):
    loads = [
        pltpu.make_async_copy(table_hbm, table_ref, sems.at[0]),
        pltpu.make_async_copy(rows_hbm, rows_ref, sems.at[1]),
        pltpu.make_async_copy(turned_hbm, turned_ref, sems.at[2]),
    ]
    loads[0].start()
    loads[0].wait()
    loads[1].start()
    loads[2].start()
    rows = jnp.concatenate([table_ref[o, LINES:VALUES, : NLAT * 16] for o in range(2)], axis=0)
    lines = lines_ref[...].reshape(NLAT * 16, LANES)
    mixed = jnp.dot(rows, lines, preferred_element_type=jnp.float32)
    mixed = mixed.astype(jnp.bfloat16).astype(jnp.float32)
    for level in range(LH):
        pick_ref[level * 64 : (level + 1) * 64, :XW] = mixed[:, level * XW : (level + 1) * XW]
    for owner in range(2):
        for v in range(NV):
            for row in range(ROWS):
                start = (owner * NV + v) * ROWS + row
                column = owner * COLS + row * XW
                grid_ref[v * LH : (v + 1) * LH, column : column + XW] = pick_ref[
                    pl.ds(start, LH, stride=64), :
                ][:, :XW]
    for owner in range(2):
        fill_stencil(table_ref, owner, stencil_ref)
        points = grid_ref[:, owner * COLS : (owner + 1) * COLS].astype(jnp.bfloat16)
        columns = jnp.dot(points, stencil_ref[owner], preferred_element_type=jnp.float32)
        out_ref[owner : owner + 1, :] = jnp.sum(
            columns * table_ref[owner, :LINES, :].astype(jnp.float32), axis=0, keepdims=True
        )
    loads[1].wait()
    loads[2].wait()


def observe(table, rows, turned, lines):
    hbm = pl.BlockSpec(memory_space=pltpu.HBM)
    vmem = pl.BlockSpec(memory_space=pltpu.VMEM)
    return pl.pallas_call(
        observe_kernel,
        in_specs=[hbm, hbm, hbm, vmem],
        out_specs=[vmem] * 4,
        out_shape=[
            pltpu.VMEM((2, REPORTS), jnp.float32),
            pltpu.VMEM(table.shape, jnp.bfloat16),
            pltpu.VMEM(rows.shape, jnp.bfloat16),
            pltpu.VMEM(turned.shape, jnp.bfloat16),
        ],
        scratch_shapes=[
            pltpu.VMEM((2, COLS, REPORTS), jnp.bfloat16),
            pltpu.VMEM((LH * 64, 128), jnp.float32),
            pltpu.VMEM((NV * LH, 2 * COLS), jnp.float32),
            pltpu.SemaphoreType.DMA((3,)),
        ],
        compiler_params=pltpu.CompilerParams(vmem_limit_bytes=OBSERVE_MIB * MIB),
        cost_estimate=pl.CostEstimate(
            flops=10**9, bytes_accessed=10 * MIB, transcendentals=0
        ),
        name="observe",
    )(table, rows, turned, lines)


def spread_kernel(part_ref, peer_ref, table_ref, rows_ref, turned_ref, departure_ref, out_ref, pick_ref):
    for owner in range(2):
        value = part_ref[owner : owner + 1, :] + peer_ref[1 - owner : 2 - owner, :]
        terms = table_ref[owner, VALUES:TABLE, :].astype(jnp.float32)
        innovation, precision = [
            terms[k : k + 1] + terms[k + 1 : k + 2] + terms[k + 2 : k + 3] for k in (6, 9)
        ]
        departure = precision * (value - innovation)
        if owner == 0:
            departure_ref[...] = departure
        level = table_ref[owner, :LINES, :].astype(jnp.float32)
        pushed = (level * departure).astype(jnp.bfloat16)
        lifted = jnp.dot(pushed, turned_ref[owner], preferred_element_type=jnp.float32)
        lifted = jnp.concatenate([lifted, jnp.zeros((NV * LH, 128), jnp.float32)], axis=1)
        for v in range(NV):
            for row in range(ROWS):
                start = (owner * NV + v) * ROWS + row
                pick_ref[pl.ds(start, LH, stride=64), :] = lifted[
                    v * LH : (v + 1) * LH, row * XW : row * XW + 128
                ]
    parts = [pick_ref[level * 64 : (level + 1) * 64, :][:, :XW] for level in range(LH)]
    lines = jnp.concatenate(parts, axis=1).astype(jnp.bfloat16)
    out = jnp.dot(rows_ref[...], lines, preferred_element_type=jnp.float32)
    out_ref[...] = out.astype(jnp.bfloat16).reshape(NLAT, 16, LANES)


def spread(part, peer, held):
    vmem = pl.BlockSpec(memory_space=pltpu.VMEM)
    return pl.pallas_call(
        spread_kernel,
        in_specs=[vmem] * 5,
        out_shape=[
            jax.ShapeDtypeStruct((1, REPORTS), jnp.float32),
            jax.ShapeDtypeStruct((NLAT, 16, LANES), jnp.bfloat16),
        ],
        scratch_shapes=[pltpu.VMEM((LH * 64, 128), jnp.float32)],
        compiler_params=pltpu.CompilerParams(vmem_limit_bytes=SPREAD_MIB * MIB),
        cost_estimate=pl.CostEstimate(
            flops=10**9, bytes_accessed=10 * MIB, transcendentals=0
        ),
        name="spread",
    )(part, peer, *held)


def on_device(
    control,
    zonal_scales,
    zonal_heights,
    meridional_scales,
    meridional_heights,
    vertical_map,
    send_blocks,
    report_slot,
    report_level,
    report_corner,
    report_weight,
    innovation,
    report_precision,
):
    strip = lax.axis_index("lat")
    half = lax.axis_index("obs")
    swap = [(0, 1), (1, 0)]

    mine = jnp.concatenate(
        [
            report_slot.reshape(1, -1).astype(jnp.float32),
            report_level.reshape(1, -1).astype(jnp.float32),
            report_corner.reshape(4, -1).astype(jnp.float32),
            report_weight.reshape(4, -1),
            innovation.reshape(1, -1),
            report_precision.reshape(1, -1),
        ],
        axis=0,
    )
    other = lax.ppermute(mine, "obs", swap)
    sends = send_blocks.reshape(2, 2)
    peer_sends = lax.ppermute(sends, "obs", swap)
    where = jnp.stack([strip % 8, half]).astype(jnp.int32)
    table, spread_rows, slab, turned = prepare(
        where,
        sends,
        peer_sends,
        (zonal_scales, zonal_heights),
        (meridional_scales, meridional_heights),
        mine,
        other,
        vertical_map,
    )

    smoothed = forward_zonal(control.reshape(NV * LH * BAND, NX), zonal_scales, zonal_heights)
    lines = lax.all_to_all(smoothed, "lat", split_axis=0, concat_axis=0, tiled=True)
    lines = pltpu.with_memory_space_constraint(lines, pltpu.VMEM)
    part, *held = observe(table, spread_rows, turned, lines)
    peer = lax.ppermute(part, "obs", swap)
    departure, back = spread(part, peer, held)
    back = lax.all_to_all(back, "lat", split_axis=0, concat_axis=0, tiled=True)
    gradient = backward_zonal(slab, back)
    return departure.reshape(report_slot.shape), gradient


def solution(mesh):
    in_specs = (
        P(None, "obs", "lat", None),
        P(),
        P(),
        P(),
        P(),
        P(),
        P("lat", "obs", None, None),
        P("lat", "obs", None),
        P("lat", "obs", None),
        P("lat", "obs", None, None),
        P("lat", "obs", None, None),
        P("lat", "obs", None),
        P("lat", "obs", None),
    )
    out_specs = (P("lat", "obs", None), P(None, "obs", "lat", None))
    return jax.shard_map(
        on_device, mesh=mesh, in_specs=in_specs, out_specs=out_specs, check_vma=False
    )
```

```python
import math

import jax
import jax.numpy as jnp
from jax import lax
from jax.experimental import pallas as pl
from jax.experimental.pallas import tpu as pltpu
from jax.sharding import PartitionSpec as P

NV = 2
LH = 32
NX = 3072
NY = 512
XW = 48
BAND = 8
NLAT = 64
GROUP = 8 * XW
LANES = LH * XW
TILE = 256
HALF = NX // 2
QUARTER = NX // 4
SLAB_SUM = 2 * HALF - TILE
SLAB_DIFFERENCE = SLAB_SUM + 2 * QUARTER - TILE
SLAB = SLAB_DIFFERENCE + 2 * QUARTER - TILE
ROWS = 16
COLS = ROWS * XW
REPORTS = 2048
SLOTS = 2
BR = 4
MIB = 2**20
LINES = NV * LH
VALUES = LINES + NV * ROWS
TABLE = VALUES + 16
FORWARD_MIB = 60
BACKWARD_MIB = 30
PREPARE_MIB = 16
OBSERVE_MIB = 45
SPREAD_MIB = 16

PIECES = (
    ((0, 48), (1, 96), (2, 128)),
    ((2, 16), (3, 64), (4, 112), (5, 128)),
    ((5, 32), (6, 80), (7, 128)),
)


def gaussians(distance, scales, heights):
    total = jnp.zeros(distance.shape, jnp.float32)
    for member in range(4):
        scale = scales[member]
        total = total + heights[member] * jnp.exp(
            -distance * distance / (2.0 * scale * scale)
        ) / jnp.sqrt(math.sqrt(math.pi) * scale)
    return total


def fill_slabs(scales_ref, heights_ref, slab_ref):
    shape = (8, NX)
    turn = lax.broadcasted_iota(jnp.int32, shape, 1) - HALF - lax.broadcasted_iota(
        jnp.int32, shape, 0
    )
    offset = jnp.abs(turn)
    distance = jnp.minimum(offset, NX - offset).astype(jnp.float32)
    scales = [scales_ref[0:1, m : m + 1] for m in range(4)]
    heights = [heights_ref[0:1, m : m + 1] for m in range(4)]
    near = gaussians(distance, scales, heights).astype(jnp.bfloat16).astype(jnp.float32)
    far = jnp.concatenate([near[:, HALF:], near[:, :HALF]], axis=1)
    total = near + far
    shifted = jnp.concatenate([total[:, QUARTER:], total[:, :QUARTER]], axis=1)
    for base, low, high, length in (
        (0.5 * (near - far), 0, SLAB_SUM, HALF),
        (0.25 * (total + shifted), SLAB_SUM, SLAB_DIFFERENCE, QUARTER),
        (0.25 * (total - shifted), SLAB_DIFFERENCE, SLAB, QUARTER),
    ):
        first = HALF - length + TILE
        for pair in range(TILE // 16):
            upper = base if pair == 0 else pltpu.roll(base, 16 * pair, 1)
            lower = pltpu.roll(base, 16 * pair + 8, 1)
            both = jnp.concatenate([upper, lower], axis=0)[:, first : first + high - low]
            slab_ref[16 * pair : 16 * pair + 16, low:high] = both.astype(jnp.bfloat16)


def zonal_part(parts_ref, slab_ref, first, start, length, low, width):
    blocks = []
    for block in range(length // TILE):
        left = start + length - TILE + low - TILE * block
        blocks.append(slab_ref[:, left : left + width])
    return jnp.dot(
        parts_ref[:, first : first + length],
        jnp.concatenate(blocks, axis=0),
        preferred_element_type=jnp.float32,
    )


def zonal_quarters(parts_ref, slab_ref, low, width):
    total = zonal_part(parts_ref, slab_ref, HALF, SLAB_SUM, QUARTER, low, width)
    change = zonal_part(
        parts_ref, slab_ref, HALF + QUARTER, SLAB_DIFFERENCE, QUARTER, low, width
    )
    west = zonal_part(parts_ref, slab_ref, 0, 0, HALF, low, width)
    east = zonal_part(parts_ref, slab_ref, 0, 0, HALF, QUARTER + low, width)
    first, second = total + change, total - change
    return first + west, second + east, first - west, second - east


def zonal_split(quarters):
    first, second = quarters[0] + quarters[2], quarters[1] + quarters[3]
    pieces = (quarters[0] - quarters[2], quarters[1] - quarters[3], first + second, first - second)
    return [piece.astype(jnp.bfloat16) for piece in pieces]


def pick(tiles, shift, lane):
    result = []
    for tile, pieces in enumerate(PIECES):
        low = 128 * tile
        value = tiles[(pieces[-1][0] - shift) % 8][:, low : low + 128]
        for block, end in pieces[-2::-1]:
            value = jnp.where(lane < end, tiles[(block - shift) % 8][:, low : low + 128], value)
        result.append(value)
    return jnp.concatenate(result, axis=1)


def forward_zonal_kernel(
    scales_hbm, heights_hbm, field_hbm, out_hbm,
    scales_ref, heights_ref, slab_ref, held_ref, parts_ref, acc_ref, out_ref, load_sems, store_sems,
):
    quarter = NV * LH * BAND // 4
    chunks = [pl.ds(quarter * k, quarter) for k in range(4)]
    loads = [
        pltpu.make_async_copy(source, target, load_sems.at[k])
        for k, (source, target) in enumerate(
            [(scales_hbm, scales_ref), (heights_hbm, heights_ref)]
            + [(field_hbm.at[chunk], held_ref.at[chunk]) for chunk in chunks]
        )
    ]
    for load in loads:
        load.start()
    loads[0].wait()
    loads[1].wait()
    fill_slabs(scales_ref, heights_ref, slab_ref)
    for k, chunk in enumerate(chunks):
        loads[2 + k].wait()
        quarters = [
            held_ref[chunk, QUARTER * q : QUARTER * (q + 1)].astype(jnp.float32) for q in range(4)
        ]
        for q, piece in enumerate(zonal_split(quarters)):
            parts_ref[chunk, QUARTER * q : QUARTER * (q + 1)] = piece
    lane = lax.broadcasted_iota(jnp.int32, (16, 128), 1)
    stores = []
    for q, value in enumerate(zonal_quarters(parts_ref, slab_ref, 0, QUARTER)):
        acc_ref[q] = value.astype(jnp.bfloat16)
    for q in range(4):
        for strips in range(2):
            first = q * 16 + strips * 8
            for group in range(LH // 8):
                turned = []
                for j in range(8):
                    row = (group * 8 + j) * BAND
                    both = jnp.concatenate(
                        [
                            acc_ref[q, v * LH * BAND + row : v * LH * BAND + row + BAND,
                                    strips * GROUP : (strips + 1) * GROUP].astype(jnp.float32)
                            for v in range(NV)
                        ],
                        axis=0,
                    )
                    both = both if j == 0 else pltpu.roll(both, XW * j, 1)
                    turned.append(both.astype(jnp.bfloat16))
                for i in range(8):
                    out_ref[first + i, :, group * GROUP : (group + 1) * GROUP] = pick(
                        turned, i, lane
                    )
            store = pltpu.make_async_copy(
                out_ref.at[first : first + 8], out_hbm.at[first : first + 8], store_sems.at[first // 8]
            )
            store.start()
            stores.append(store)
    for store in stores:
        store.wait()


def forward_zonal(field, scales, heights):
    rows = NV * LH * BAND
    hbm = pl.BlockSpec(memory_space=pltpu.HBM)
    return pl.pallas_call(
        forward_zonal_kernel,
        in_specs=[hbm] * 3,
        out_specs=hbm,
        out_shape=jax.ShapeDtypeStruct((NLAT, 16, LANES), jnp.bfloat16),
        scratch_shapes=[
            pltpu.VMEM((1, 4), jnp.float32),
            pltpu.VMEM((1, 4), jnp.float32),
            pltpu.VMEM((TILE, SLAB), jnp.bfloat16),
            pltpu.VMEM((rows, NX), jnp.bfloat16),
            pltpu.VMEM((rows, NX), jnp.bfloat16),
            pltpu.VMEM((4, rows, QUARTER), jnp.bfloat16),
            pltpu.VMEM((NLAT, 16, LANES), jnp.bfloat16),
            pltpu.SemaphoreType.DMA((6,)),
            pltpu.SemaphoreType.DMA((NLAT // 8,)),
        ],
        compiler_params=pltpu.CompilerParams(vmem_limit_bytes=FORWARD_MIB * MIB),
        cost_estimate=pl.CostEstimate(
            flops=rows * NX * NX, bytes_accessed=8 * MIB, transcendentals=10**5
        ),
        name="forward_zonal",
    )(scales.reshape(1, 4), heights.reshape(1, 4), field)


def backward_zonal_kernel(
    slab_hbm, lines_ref, out_hbm, slab_ref, parts_ref, acc_ref, load_sem, sems
):
    load = pltpu.make_async_copy(slab_hbm, slab_ref, load_sem)
    load.start()
    lane = lax.broadcasted_iota(jnp.int32, (16, 128), 1)

    def levels(strips, group):
        tiles = [
            lines_ref[strips * 8 + i, :, group * GROUP : (group + 1) * GROUP] for i in range(8)
        ]
        picked = [pick(tiles, j, lane).astype(jnp.float32) for j in range(8)]
        return [p if j == 0 else pltpu.roll(p, GROUP - XW * j, 1) for j, p in enumerate(picked)]

    def fill(strips):
        for group in range(LH // 8):
            quarters = [levels(strips + NLAT // 32 * q, group) for q in range(4)]
            for j in range(8):
                row = (group * 8 + j) * 16
                for q, piece in enumerate(zonal_split([quarter[j] for quarter in quarters])):
                    start = strips * GROUP + q * QUARTER
                    parts_ref[row : row + 16, start : start + GROUP] = piece

    for strips in range(NLAT // 32):
        fill(strips)
    load.wait()
    stores = []
    for step in range(QUARTER // TILE):
        low = step * TILE
        for q, value in enumerate(zonal_quarters(parts_ref, slab_ref, low, TILE)):
            for level in range(LH):
                for v in range(NV):
                    row = (level * NV + v) * BAND
                    acc_ref[step, q, v, level] = value[row : row + BAND]
        for q in range(4):
            left = q * QUARTER + low
            store = pltpu.make_async_copy(
                acc_ref.at[step, q], out_hbm.at[:, :, :, left : left + TILE], sems.at[step, q]
            )
            store.start()
            stores.append(store)
    for store in stores:
        store.wait()


def backward_zonal(slab, lines):
    rows = NV * LH * BAND
    hbm = pl.BlockSpec(memory_space=pltpu.HBM)
    return pl.pallas_call(
        backward_zonal_kernel,
        in_specs=[hbm, pl.BlockSpec(memory_space=pltpu.VMEM)],
        out_specs=hbm,
        out_shape=jax.ShapeDtypeStruct((NV, LH, BAND, NX), jnp.float32),
        scratch_shapes=[
            pltpu.VMEM((TILE, SLAB), jnp.bfloat16),
            pltpu.VMEM((rows, NX), jnp.bfloat16),
            pltpu.VMEM((QUARTER // TILE, 4, NV, LH, BAND, TILE), jnp.float32),
            pltpu.SemaphoreType.DMA,
            pltpu.SemaphoreType.DMA((QUARTER // TILE, 4)),
        ],
        compiler_params=pltpu.CompilerParams(vmem_limit_bytes=BACKWARD_MIB * MIB),
        cost_estimate=pl.CostEstimate(
            flops=rows * NX * NX, bytes_accessed=12 * MIB, transcendentals=0
        ),
        name="backward_zonal",
    )(slab, lines)


def fill_stencil(table_ref, owner, stencil_ref):
    chunk = 256
    for low in range(0, REPORTS, chunk):
        part = slice(low, low + chunk)
        values = table_ref[owner, VALUES:TABLE, part].astype(jnp.float32)
        corner = values[1:2].astype(jnp.int32)
        first = values[0:1].astype(jnp.int32) * BR + corner // XW
        cell = lax.rem(corner, XW)
        column = lax.broadcasted_iota(jnp.int32, (XW, chunk), 0)
        west, east = column == cell, column == cell + 1
        lower, upper = [
            jnp.where(west, values[c : c + 1], jnp.where(east, values[c + 1 : c + 2], 0.0))
            for c in (2, 4)
        ]
        for row in range(ROWS):
            value = jnp.where(first == row, lower, jnp.where(first == row - 1, upper, 0.0))
            stencil_ref[owner, row * XW : (row + 1) * XW, part] = value.astype(jnp.bfloat16)


def prepare_kernel(
    where_ref, sends_ref, peer_sends_ref, zonal_scales_ref, zonal_heights_ref, scales_ref, heights_ref,
    mine_ref, other_ref, map_ref, table_ref, spread_ref, slab_ref, turned_ref, column_ref,
):
    fill_slabs(zonal_scales_ref, zonal_heights_ref, slab_ref)
    strip_turn, half = where_ref[0], where_ref[1]
    shape = (LH, 2 * LH)
    slot = lax.broadcasted_iota(jnp.int32, shape, 0)
    level = (slot // 8) * 8 + lax.rem(lax.rem(slot, 8) + (8 - strip_turn), 8) + LH * half
    order = (lax.broadcasted_iota(jnp.int32, shape, 1) == level).astype(jnp.bfloat16)
    row = lax.broadcasted_iota(jnp.int32, (64, 128), 0)
    place = lax.rem(row, 4)
    for owner in range(2):
        target = half if owner == 0 else 1 - half
        for source in range(2):
            for turn in range(SLOTS):
                block = jnp.where(
                    half == source, sends_ref[target, turn], peer_sends_ref[target, turn]
                )
                chosen = (row // 32 == owner) & (
                    lax.rem(row // 4, 4) == source * SLOTS + turn
                )
                place = place + jnp.where(chosen, source * (NY // 2) + block * 4, 0)
    line = lax.broadcasted_iota(jnp.int32, (64, NLAT * 16), 1)
    apart = jnp.abs(place[:, :1] - ((line // 16) * BAND + lax.rem(line, BAND))).astype(jnp.float32)
    matrix = gaussians(
        apart,
        [scales_ref[0:1, m : m + 1] for m in range(4)],
        [heights_ref[0:1, m : m + 1] for m in range(4)],
    )
    own = lax.rem(row // ROWS, NV)[:, :1] == lax.rem(line // BAND, NV)
    matrix = jnp.where(own, matrix, 0.0)
    spread_ref[...] = matrix.T.astype(jnp.bfloat16)
    matrix = matrix.astype(jnp.bfloat16)
    blank = jnp.zeros((NV * ROWS, REPORTS - NLAT * 16), jnp.bfloat16)
    for owner in range(2):
        table_ref[owner, LINES:VALUES, : NLAT * 16] = matrix[owner * 32 : (owner + 1) * 32]
        table_ref[owner, LINES:VALUES, NLAT * 16 :] = blank
    for owner, ref in enumerate((mine_ref, other_ref)):
        code = ref[1:2, :].astype(jnp.int32)
        for v in range(NV):
            rows = lax.broadcasted_iota(jnp.int32, (2 * LH, REPORTS), 0) + 2 * LH * v
            hot = (rows == code).astype(jnp.float32).astype(jnp.bfloat16)
            picked = lax.dot_general(
                map_ref[v], hot, (((0,), (0,)), ((), ())), preferred_element_type=jnp.float32
            ).astype(jnp.bfloat16)
            table_ref[owner, v * LH : (v + 1) * LH, :] = jnp.dot(
                order, picked, preferred_element_type=jnp.float32
            ).astype(jnp.bfloat16)
        values = [ref[0:1, :], ref[2:3, :], ref[6:10, :]]
        for row in (10, 11):
            rest = ref[row : row + 1, :]
            for _ in range(3):
                term = rest.astype(jnp.bfloat16).astype(jnp.float32)
                values.append(term)
                rest = rest - term
        values.append(jnp.zeros((4, REPORTS), jnp.float32))
        values = jnp.concatenate(values, axis=0)
        table_ref[owner, VALUES:TABLE, :] = values.astype(jnp.bfloat16)
        column_ref[...] = values.T

        def turn_stencil(step, carry):
            start = pl.multiple_of(step * 128, 128)
            columns = column_ref[pl.ds(start, 128), :]
            point = (columns[:, 0:1] * float(BR * XW) + columns[:, 1:2]).astype(jnp.int32)
            apart = lax.broadcasted_iota(jnp.int32, (128, COLS), 1) - point
            value = jnp.zeros((128, COLS), jnp.float32)
            for c, offset in enumerate((0, 1, XW, XW + 1)):
                value = jnp.where(apart == offset, columns[:, 2 + c : 3 + c], value)
            turned_ref[owner, pl.ds(start, 128), :] = value.astype(jnp.bfloat16)
            return carry

        lax.fori_loop(0, REPORTS // 128, turn_stencil, 0)


def prepare(where, sends, peer_sends, zonal, meridional, mine, other, vertical_map):
    smem = pl.BlockSpec(memory_space=pltpu.SMEM)
    vmem = pl.BlockSpec(memory_space=pltpu.VMEM)
    return pl.pallas_call(
        prepare_kernel,
        in_specs=[smem] * 3 + [vmem] * 7,
        out_shape=[
            jax.ShapeDtypeStruct((2, TABLE, REPORTS), jnp.bfloat16),
            jax.ShapeDtypeStruct((NLAT * 16, 64), jnp.bfloat16),
            jax.ShapeDtypeStruct((TILE, SLAB), jnp.bfloat16),
            jax.ShapeDtypeStruct((2, REPORTS, COLS), jnp.bfloat16),
        ],
        scratch_shapes=[pltpu.VMEM((REPORTS, 16), jnp.float32)],
        compiler_params=pltpu.CompilerParams(vmem_limit_bytes=PREPARE_MIB * MIB),
        cost_estimate=pl.CostEstimate(
            flops=10**9, bytes_accessed=8 * MIB, transcendentals=3 * 10**5
        ),
        name="prepare",
    )(where, sends, peer_sends, *[x.reshape(1, 4) for x in zonal + meridional], mine, other, vertical_map)


def observe_kernel(
    table_hbm, rows_hbm, turned_hbm, lines_ref, out_ref, table_ref, rows_ref, turned_ref,
    stencil_ref, pick_ref, grid_ref, sems,
):
    loads = [
        pltpu.make_async_copy(table_hbm, table_ref, sems.at[0]),
        pltpu.make_async_copy(rows_hbm, rows_ref, sems.at[1]),
        pltpu.make_async_copy(turned_hbm, turned_ref, sems.at[2]),
    ]
    loads[0].start()
    loads[0].wait()
    loads[1].start()
    loads[2].start()
    rows = jnp.concatenate([table_ref[o, LINES:VALUES, : NLAT * 16] for o in range(2)], axis=0)
    lines = lines_ref[...].reshape(NLAT * 16, LANES)
    mixed = jnp.dot(rows, lines, preferred_element_type=jnp.float32)
    mixed = mixed.astype(jnp.bfloat16).astype(jnp.float32)
    for level in range(LH):
        pick_ref[level * 64 : (level + 1) * 64, :XW] = mixed[:, level * XW : (level + 1) * XW]
    for owner in range(2):
        for v in range(NV):
            for row in range(ROWS):
                start = (owner * NV + v) * ROWS + row
                column = owner * COLS + row * XW
                grid_ref[v * LH : (v + 1) * LH, column : column + XW] = pick_ref[
                    pl.ds(start, LH, stride=64), :
                ][:, :XW]
    for owner in range(2):
        fill_stencil(table_ref, owner, stencil_ref)
        points = grid_ref[:, owner * COLS : (owner + 1) * COLS].astype(jnp.bfloat16)
        columns = jnp.dot(points, stencil_ref[owner], preferred_element_type=jnp.float32)
        out_ref[owner : owner + 1, :] = jnp.sum(
            columns * table_ref[owner, :LINES, :].astype(jnp.float32), axis=0, keepdims=True
        )
    loads[1].wait()
    loads[2].wait()


def observe(table, rows, turned, lines):
    hbm = pl.BlockSpec(memory_space=pltpu.HBM)
    vmem = pl.BlockSpec(memory_space=pltpu.VMEM)
    return pl.pallas_call(
        observe_kernel,
        in_specs=[hbm, hbm, hbm, vmem],
        out_specs=[vmem] * 4,
        out_shape=[
            pltpu.VMEM((2, REPORTS), jnp.float32),
            pltpu.VMEM(table.shape, jnp.bfloat16),
            pltpu.VMEM(rows.shape, jnp.bfloat16),
            pltpu.VMEM(turned.shape, jnp.bfloat16),
        ],
        scratch_shapes=[
            pltpu.VMEM((2, COLS, REPORTS), jnp.bfloat16),
            pltpu.VMEM((LH * 64, 128), jnp.float32),
            pltpu.VMEM((NV * LH, 2 * COLS), jnp.float32),
            pltpu.SemaphoreType.DMA((3,)),
        ],
        compiler_params=pltpu.CompilerParams(vmem_limit_bytes=OBSERVE_MIB * MIB),
        cost_estimate=pl.CostEstimate(
            flops=10**9, bytes_accessed=10 * MIB, transcendentals=0
        ),
        name="observe",
    )(table, rows, turned, lines)


def spread_kernel(part_ref, peer_ref, table_ref, rows_ref, turned_ref, departure_ref, out_ref, pick_ref):
    for owner in range(2):
        value = part_ref[owner : owner + 1, :] + peer_ref[1 - owner : 2 - owner, :]
        terms = table_ref[owner, VALUES:TABLE, :].astype(jnp.float32)
        innovation, precision = [
            terms[k : k + 1] + terms[k + 1 : k + 2] + terms[k + 2 : k + 3] for k in (6, 9)
        ]
        departure = precision * (value - innovation)
        if owner == 0:
            departure_ref[...] = departure
        level = table_ref[owner, :LINES, :].astype(jnp.float32)
        pushed = (level * departure).astype(jnp.bfloat16)
        lifted = jnp.dot(pushed, turned_ref[owner], preferred_element_type=jnp.float32)
        lifted = jnp.concatenate([lifted, jnp.zeros((NV * LH, 128), jnp.float32)], axis=1)
        for v in range(NV):
            for row in range(ROWS):
                start = (owner * NV + v) * ROWS + row
                pick_ref[pl.ds(start, LH, stride=64), :] = lifted[
                    v * LH : (v + 1) * LH, row * XW : row * XW + 128
                ]
    parts = [pick_ref[level * 64 : (level + 1) * 64, :][:, :XW] for level in range(LH)]
    lines = jnp.concatenate(parts, axis=1).astype(jnp.bfloat16)
    out = jnp.dot(rows_ref[...], lines, preferred_element_type=jnp.float32)
    out_ref[...] = out.astype(jnp.bfloat16).reshape(NLAT, 16, LANES)


def spread(part, peer, held):
    vmem = pl.BlockSpec(memory_space=pltpu.VMEM)
    return pl.pallas_call(
        spread_kernel,
        in_specs=[vmem] * 5,
        out_shape=[
            jax.ShapeDtypeStruct((1, REPORTS), jnp.float32),
            jax.ShapeDtypeStruct((NLAT, 16, LANES), jnp.bfloat16),
        ],
        scratch_shapes=[pltpu.VMEM((LH * 64, 128), jnp.float32)],
        compiler_params=pltpu.CompilerParams(vmem_limit_bytes=SPREAD_MIB * MIB),
        cost_estimate=pl.CostEstimate(
            flops=10**9, bytes_accessed=10 * MIB, transcendentals=0
        ),
        name="spread",
    )(part, peer, *held)


def on_device(
    control,
    zonal_scales,
    zonal_heights,
    meridional_scales,
    meridional_heights,
    vertical_map,
    send_blocks,
    report_slot,
    report_level,
    report_corner,
    report_weight,
    innovation,
    report_precision,
):
    strip = lax.axis_index("lat")
    half = lax.axis_index("obs")
    swap = [(0, 1), (1, 0)]

    mine = jnp.concatenate(
        [
            report_slot.reshape(1, -1).astype(jnp.float32),
            report_level.reshape(1, -1).astype(jnp.float32),
            report_corner.reshape(4, -1).astype(jnp.float32),
            report_weight.reshape(4, -1),
            innovation.reshape(1, -1),
            report_precision.reshape(1, -1),
        ],
        axis=0,
    )
    other = lax.ppermute(mine, "obs", swap)
    sends = send_blocks.reshape(2, 2)
    peer_sends = lax.ppermute(sends, "obs", swap)
    where = jnp.stack([strip % 8, half]).astype(jnp.int32)
    table, spread_rows, slab, turned = prepare(
        where,
        sends,
        peer_sends,
        (zonal_scales, zonal_heights),
        (meridional_scales, meridional_heights),
        mine,
        other,
        vertical_map,
    )

    smoothed = forward_zonal(control.reshape(NV * LH * BAND, NX), zonal_scales, zonal_heights)
    lines = lax.all_to_all(smoothed, "lat", split_axis=0, concat_axis=0, tiled=True)
    lines = pltpu.with_memory_space_constraint(lines, pltpu.VMEM)
    part, *held = observe(table, spread_rows, turned, lines)
    peer = lax.ppermute(part, "obs", swap)
    departure, back = spread(part, peer, held)
    back = lax.all_to_all(back, "lat", split_axis=0, concat_axis=0, tiled=True)
    gradient = backward_zonal(slab, back)
    return departure.reshape(report_slot.shape), gradient


def solution(mesh):
    in_specs = (
        P(None, "obs", "lat", None),
        P(),
        P(),
        P(),
        P(),
        P(),
        P("lat", "obs", None, None),
        P("lat", "obs", None),
        P("lat", "obs", None),
        P("lat", "obs", None, None),
        P("lat", "obs", None, None),
        P("lat", "obs", None),
        P("lat", "obs", None),
    )
    out_specs = (P("lat", "obs", None), P(None, "obs", "lat", None))
    return jax.shard_map(
        on_device, mesh=mesh, in_specs=in_specs, out_specs=out_specs, check_vma=False
    )
```
